32 devices in a mesh: dp: 16 (over z, x, core), mp: 2 (over y).
Axes of the slice: x: 2, y: 2, z: 4, core: 2. Of those that a mesh axis runs over, the one named last changes fastest.
Arguments:
- tokens: bfloat16 [24576, 1024], P('dp', 'mp'), may hold values from -6 to 6
- out_grad: bfloat16 [24576, 1024], P('dp', 'mp'), may hold values from -0.1875 to 0.1875
- master: float32 [2, 256, 128, 128], P('mp', 'dp'), may hold values from -0.1875 to 0.1875
- momentum: float32 [2, 256, 128, 128], P('mp', 'dp'), may hold values from -6 to 6
- residual: bfloat16 [16, 2, 256, 128, 128], P('dp', 'mp'), may hold values from -1.75 to 1.75
- kept_blocks: int32 [16, 2, 64], P('dp', 'mp'), may hold values from 0 to 255, as said below
Outputs:
- new_master: float32 [2, 256, 128, 128], P('mp', 'dp')
- new_momentum: float32 [2, 256, 128, 128], P('mp', 'dp')
- new_residual: bfloat16 [16, 2, 256, 128, 128], P('dp', 'mp')
The draws below stay inside these ranges and needn't reach their ends.
Inputs may be any that keep to these rules, and one draw needn't show every extreme that they name: `kept_blocks`: each list names 64 distinct blocks of its shard.
All inputs are finite; a program needn't handle non-finite values.
Results may differ from the reference program's by a relative error of at most 0.0058.
Values may be sent and summed in bfloat16 or wider, within the bound.
No kernel may reach another device: no remote copies, remote signals or barrier semaphores. Data moves between devices by JAX's collectives and lax.ppermute only.
A program may use at most 128 MiB of HBM per device.

```python
import jax
import jax.numpy as jnp
from jax import lax

D = 1024
TOK_DEV = 1536
TILE = 128
REPLICAS = 16
SHARDS = 2
TOKENS = 24576
FFS = 2048
BLOCKS = 256
KEEP = 64


def draw_kept_blocks(key, part):
    key = jax.random.fold_in(key, 7)
    popular = jax.random.randint(jax.random.fold_in(key, 1), (BLOCKS,), 0, 8)
    noise = jax.random.randint(jax.random.fold_in(key, 2), (REPLICAS, SHARDS, BLOCKS), 0, 8)
    scores = (popular[None, None, :] + noise) * BLOCKS + jnp.arange(BLOCKS, dtype=jnp.int32)[None, None, :]
    picked = lax.top_k(scores, KEEP)[1]
    return picked.astype(jnp.int32)


def block_scale(rng, extent, shards, least, top_value):
    def one(dim, parts):
        steps = jax.random.uniform(jax.random.fold_in(jax.random.fold_in(rng, 6), dim), (parts,), jnp.float32, least / len(shards), top_value / len(shards))
        return jnp.repeat(jnp.exp(steps), extent[dim] // parts).reshape((-1,) + (1,) * (len(extent) - dim - 1))

    loudness = one(*shards[0])
    for cut in shards[1:]:
        loudness = loudness * one(*cut)
    return loudness


def scatter_about(key, extent, width, limit, pieces=(), held_as=jnp.bfloat16):
    values = jax.random.normal(key, extent, jnp.float32) * width
    if len(pieces) > 0:
        values = block_scale(key, extent, pieces, -0.22, 0.18) * values
    return jnp.clip(values, min=-limit, max=limit).astype(held_as)


def setup_inputs(seed: int = 0) -> dict:
    streams_of = jax.random.split(jax.random.key(seed), 7)
    tokens = scatter_about(streams_of[0], (TOKENS, D), 1.0, 6.0, ((0, 16), (1, 2)))
    out_grad = scatter_about(streams_of[1], (TOKENS, D), 0.03, 0.1875, ((0, 16), (1, 2)))
    master = scatter_about(streams_of[2], (SHARDS, BLOCKS, TILE, TILE), D ** -0.5, 0.1875, ((0, 2), (1, 16)), jnp.float32)
    momentum = scatter_about(streams_of[3], (SHARDS, BLOCKS, TILE, TILE), 1.0, 6.0, ((0, 2), (1, 16)), jnp.float32)
    residual = scatter_about(streams_of[4], (REPLICAS, SHARDS, BLOCKS, TILE, TILE), 0.3, 1.75, ((0, 16), (1, 2)))
    kept_blocks = draw_kept_blocks(jax.random.fold_in(streams_of[6], 71), 0)
    return {"tokens": tokens, "out_grad": out_grad, "master": master, "momentum": momentum, "residual": residual, "kept_blocks": kept_blocks}


momentum_decay = 0.9
step_size = 0.01

def activation(values):
    return jax.nn.gelu(values, approximate=True)

def to_blocks(matrix, tile_size):
    rows, cols = matrix.shape
    blocked = matrix.reshape(rows // tile_size, tile_size, cols // tile_size, tile_size)
    return blocked.transpose(0, 2, 1, 3).reshape(-1, tile_size, tile_size)

def from_blocks(blocks, rows, cols, tile_size):
    blocked = blocks.reshape(rows // tile_size, cols // tile_size, tile_size, tile_size)
    return blocked.transpose(0, 2, 1, 3).reshape(rows, cols)

def reference(tokens, out_grad, master, momentum, residual, kept_blocks):
    half_count = BLOCKS // 2
    block_ids = jnp.arange(BLOCKS, dtype=jnp.int32)
    masters = []
    moments = []
    leftover_list = []
    for shard_index in range(SHARDS):
        working = master[shard_index].astype(jnp.bfloat16)
        first_layer_weight = from_blocks(working[:half_count], D, FFS, TILE)
        second_layer_weight = from_blocks(working[half_count:], FFS, D, TILE)

        def replica_step(total, replica):
            start = (replica * TOK_DEV).astype(jnp.int32)
            inputs = lax.dynamic_slice_in_dim(tokens, start, TOK_DEV, 0)
            grads_out = lax.dynamic_slice_in_dim(out_grad, start, TOK_DEV, 0)
            pre = jnp.dot(inputs, first_layer_weight, preferred_element_type=jnp.float32)
            act_full, pullback = jax.vjp(activation, pre)
            act = act_full.astype(jnp.bfloat16)
            act_grad = jnp.dot(grads_out, second_layer_weight.T, preferred_element_type=jnp.float32)
            hidden_gradient = pullback(act_grad)[0].astype(jnp.bfloat16)
            first_layer_gradient = jnp.dot(inputs.T, hidden_gradient, preferred_element_type=jnp.float32)
            second_g = jnp.dot(act.T, grads_out, preferred_element_type=jnp.float32)
            stored = lax.dynamic_index_in_dim(residual, replica, 0, keepdims=False)[shard_index]
            grad_full = jnp.concatenate([to_blocks(first_layer_gradient, TILE), to_blocks(second_g, TILE)], axis=0)
            grad_full = grad_full + stored.astype(jnp.float32)
            chosen = lax.dynamic_index_in_dim(kept_blocks, replica, 0, keepdims=False)[shard_index]
            flags = jnp.any(block_ids[None, :] == chosen[:, None], axis=0)[:, None, None]
            leftover = jnp.where(flags, 0.0, grad_full).astype(jnp.bfloat16)
            return (total + jnp.where(flags, grad_full, 0.0), leftover)
        start_total = jnp.zeros((BLOCKS, TILE, TILE), jnp.float32)
        block_sum, leftovers = lax.scan(replica_step, start_total, jnp.arange(REPLICAS, dtype=jnp.int32))
        new_mom = momentum_decay * momentum[shard_index] + block_sum
        masters.append(master[shard_index] - step_size * new_mom)
        moments.append(new_mom)
        leftover_list.append(leftovers)
    return (jnp.stack(masters), jnp.stack(moments), jnp.stack(leftover_list, axis=1))
```

```python
import functools

import jax
import jax.numpy as jnp
from jax import lax
from jax.experimental import pallas as pl
from jax.experimental.pallas import tpu as pltpu
from jax.sharding import PartitionSpec as P

momentum_decay = 0.9
step_size = 0.01
BF = jnp.bfloat16
F32 = jnp.float32
ANY = pl.BlockSpec(memory_space=pl.ANY)
GELU_S = 0.7978845608028654
GELU_C = 0.044715


def activation(values):
    return jax.nn.gelu(values, approximate=True)


def gelu_and_slope(v):
    sq = v * v
    t = jnp.tanh(v * (GELU_S + (GELU_S * GELU_C) * sq))
    half = 0.5 + 0.5 * t
    act = v * half
    slope = half + act * (1.0 - t) * (GELU_S + (3.0 * GELU_S * GELU_C) * sq)
    return act, slope


def unit_copies(owner, half, src, dst, sem, first, shift):
    if first:
        row = pl.multiple_of(((owner - shift) & 7) * 128, 128)
        lo, n = (0, 16) if half is None else (8 * half, 8)
        return [pltpu.make_async_copy(src, dst.at[pl.ds(lo, n), pl.ds(row, 128)], sem)]
    out = []
    for i in range(2):
        if half is None or half == i:
            row = pl.multiple_of((owner - 8) * 256 + 128 * i, 128)
            part = src.at[pl.ds(8 * i, 8)] if half is None else src
            out.append(pltpu.make_async_copy(part, dst.at[:, pl.ds(row, 128)], sem))
    return out


def load_weight(halves, first, owners, shift, srcs, dst, sem):
    for s, src in enumerate(srcs):
        owner = owners[s]

        @pl.when((owner < 8) if first else (owner >= 8))
        def _():
            for copy in unit_copies(owner, halves[s], src, dst, sem, first, shift):
                copy.start()


def pre_kernel(halves, owners, x_own, x_other, *refs):
    n = len(halves)
    srcs, (xa, slope_ref, w1, sem) = refs[:n], refs[n:]
    step = pl.program_id(0)
    shift = owners[n]

    @pl.when(step == 0)
    def _():
        load_weight(halves, True, owners, shift, srcs, w1, sem)

    for s in range(4):

        @pl.when(step == s)
        def _(s=s):
            src = x_own if s < 2 else x_other
            xa[...] = src[:, 256 * (s % 2) : 256 * (s % 2) + 256]

    @pl.when(step == 3)
    def _():
        pltpu.make_async_copy(w1, w1, sem).wait()

    @pl.when(step >= 4)
    def _():
        c = 2 * (step - 4)
        w = jnp.concatenate([w1[c], w1[c + 1]], axis=1)
        half = w.shape[0] // 2
        rows = x_own.shape[0]
        for r in range(0, rows, 512):
            pre = jnp.dot(x_own[r : r + 512, :], w[:half], preferred_element_type=F32)
            pre += jnp.dot(x_other[r : r + 512, :], w[half:], preferred_element_type=F32)
            act, slope = gelu_and_slope(pre)
            xa[r : r + 512, :] = act.astype(BF)
            slope_ref[r : r + 512, :] = slope


def hid_kernel(halves, owners, dy_own, dy_other, slope_ref, *refs):
    n = len(halves)
    srcs, rest = refs[:n], refs[n:]
    hd, w2, sem = rest[-3:]
    step = pl.program_id(0)
    shift = owners[n]

    @pl.when(step == 0)
    def _():
        load_weight(halves, False, owners, shift, srcs, w2, sem)

    for s in range(4):

        @pl.when(step == s)
        def _(s=s):
            src = dy_own if s < 2 else dy_other
            hd[...] = src[:, 256 * (s % 2) : 256 * (s % 2) + 256]

    @pl.when(step == 3)
    def _():
        pltpu.make_async_copy(w2, w2, sem).wait()

    @pl.when(step >= 4)
    def _():
        row = pl.multiple_of(256 * (step - 4), 256)
        w = jnp.concatenate([w2[(c + shift) & 7, pl.ds(row, 256), :] for c in range(8)], axis=1)
        half = w.shape[1] // 2
        dims = (((1,), (1,)), ((), ()))
        g = lax.dot_general(dy_own[...], w[:, :half], dims, preferred_element_type=F32)
        g += lax.dot_general(dy_other[...], w[:, half:], dims, preferred_element_type=F32)
        hd[...] = (g * slope_ref[...]).astype(BF)


def grad_kernel(info, flags, a_ref, b_ref, res_ref, *refs):
    new_res, mine, other = refs[-3:]
    group, h = pl.program_id(0), pl.program_id(1)
    g = info[3 * group]
    first = g < 4
    shift, core = info[info.shape[0] - 2], info[info.shape[0] - 1]
    grad = lax.dot_general(a_ref[...], b_ref[...], (((0,), (0,)), ((), ())), preferred_element_type=F32)
    for i in range(2):
        for j in range(8):
            slot = jnp.where(first, 8 * h + j, 8 * i + ((j + shift) & 7))
            target = jnp.where(first, i, h)
            flat = 16 * target + slot
            kept = flags[32 * g + flat] != 0
            v = grad[128 * i : 128 * i + 128, 128 * j : 128 * j + 128] + res_ref[0, flat].astype(F32)
            new_res[0, flat] = jnp.where(kept, 0.0, v).astype(BF)
            send = jnp.where(kept, v, 0.0).astype(BF)

            @pl.when(target == core)
            def _(send=send, slot=slot):
                mine[0, slot] = send

            @pl.when(target != core)
            def _(send=send, slot=slot):
                other[0, slot] = send


def run_pre(owners, halves, x_own, x_other, units):
    rows = x_own.shape[0]
    full = pl.BlockSpec(x_own.shape, lambda i, *_: (0, 0))
    return pl.pallas_call(
        functools.partial(pre_kernel, halves),
        grid_spec=pltpu.PrefetchScalarGridSpec(
            num_scalar_prefetch=1,
            grid=(12,),
            in_specs=[full, full] + [ANY] * len(units),
            out_specs=[
                pl.BlockSpec((rows, 256), lambda i, *_: (0, i)),
                pl.BlockSpec((rows, 256), lambda i, *_: (0, jnp.maximum(i - 4, 0))),
            ],
            scratch_shapes=[pltpu.VMEM((16, 1024, 128), BF), pltpu.SemaphoreType.DMA],
        ),
        out_shape=[jax.ShapeDtypeStruct((rows, 3072), BF), jax.ShapeDtypeStruct((rows, 2048), F32)],
        compiler_params=pltpu.CompilerParams(vmem_limit_bytes=40 * 2**20),
        cost_estimate=pl.CostEstimate(flops=2 * rows * 1024 * 2048, bytes_accessed=30_000_000, transcendentals=rows * 2048),
        name="pre_act",
    )(owners, x_own, x_other, *units)


def run_hid(owners, halves, dy_own, dy_other, slope, units, row_block, hd=None):
    rows = dy_own.shape[0]
    total = slope.shape[0]
    full = pl.BlockSpec(dy_own.shape, lambda i, *_: (0, 0))
    operands = [owners, dy_own, dy_other, slope, *units]
    specs = [full, full, pl.BlockSpec((rows, 256), lambda i, *_: (row_block, jnp.maximum(i - 4, 0)))] + [ANY] * len(units)
    alias = {}
    if hd is not None:
        alias = {len(operands): 0}
        operands.append(hd)
        specs.append(ANY)
    return pl.pallas_call(
        functools.partial(hid_kernel, halves),
        grid_spec=pltpu.PrefetchScalarGridSpec(
            num_scalar_prefetch=1,
            grid=(12,),
            in_specs=specs,
            out_specs=pl.BlockSpec((rows, 256), lambda i, *_: (row_block, jnp.where(i < 4, i + 8, i - 4))),
            scratch_shapes=[pltpu.VMEM((8, 2048, 128), BF), pltpu.SemaphoreType.DMA],
        ),
        out_shape=jax.ShapeDtypeStruct((total, 3072), BF),
        input_output_aliases=alias,
        compiler_params=pltpu.CompilerParams(vmem_limit_bytes=40 * 2**20),
        cost_estimate=pl.CostEstimate(flops=2 * rows * 1024 * 2048, bytes_accessed=30_000_000 * rows // total, transcendentals=0),
        name="hid_grad",
    )(*operands)


def run_grads(info, flags, xa, hd, residual, new_res, count):
    rows = xa.shape[0]
    operands = [info, flags, xa, hd, residual]
    block = lambda size: pl.BlockSpec((1, size, 128, 128), lambda i, h, info, *_: (info[3 * i], 0, 0, 0))
    local_block = pl.BlockSpec((1, 16, 128, 128), lambda i, h, *_: (i, 0, 0, 0))
    specs = [
        pl.BlockSpec((rows, 256), lambda i, h, info, *_: (0, jnp.where(info[3 * i] < 4, info[3 * i + 1], info[3 * i + 1] + h))),
        pl.BlockSpec((rows, 1024), lambda i, h, info, *_: (0, jnp.where(info[3 * i] < 4, h, 2))),
        block(32),
    ]
    alias = {}
    if new_res is not None:
        alias = {len(operands): 0}
        operands.append(new_res)
        specs.append(ANY)
    sent = jax.ShapeDtypeStruct((count, 16, 128, 128), BF)
    return pl.pallas_call(
        grad_kernel,
        grid_spec=pltpu.PrefetchScalarGridSpec(
            num_scalar_prefetch=2,
            grid=(count, 2),
            in_specs=specs,
            out_specs=[block(32), local_block, local_block],
        ),
        out_shape=[jax.ShapeDtypeStruct(residual.shape, BF), sent, sent],
        input_output_aliases=alias,
        compiler_params=pltpu.CompilerParams(vmem_limit_bytes=40 * 2**20),
        cost_estimate=pl.CostEstimate(flops=2 * rows * 1024 * 512 * count, bytes_accessed=12_000_000 * count, transcendentals=0),
        name="grad_blocks",
    )(*operands)


def chip_at(place):
    place = place % 8
    if isinstance(place, int):
        return 2 * place if place < 4 else 2 * (7 - place) + 1
    return jnp.where(place < 4, 2 * place, 2 * (7 - place) + 1)


def ring_pairs(step):
    return [(2 * chip_at(p) + c, 2 * chip_at(p + step) + c) for p in range(8) for c in range(2)]


UP, DOWN = ring_pairs(1), ring_pairs(-1)
CORES = [(i, i ^ 1) for i in range(16)]
PAIR = [(0, 1), (1, 0)]


def hop(array, pairs):
    return lax.ppermute(array, "dp", pairs)


def local_ring(tokens, out_grad, master, momentum, residual, kept_blocks):
    mine = lax.axis_index("dp").astype(jnp.int32)
    shard = lax.axis_index("mp").astype(jnp.int32)
    core = mine & 1
    chip = mine >> 1
    place = jnp.where((chip & 1) == 0, chip >> 1, 7 - (chip >> 1))
    rows = tokens.shape[0]

    x_other = lax.ppermute(tokens, "mp", PAIR)
    parts = 2
    size = rows // parts
    dy_own = [out_grad[i * size : (i + 1) * size] for i in range(parts)]
    dy_other = [lax.ppermute(t, "mp", PAIR) for t in dy_own]

    own = master[0].astype(BF)
    up1, down1 = hop(own, UP), hop(own, DOWN)
    up2, down2 = hop(up1, UP), hop(down1, DOWN)
    up3, down3 = hop(up2, UP), hop(down2, DOWN)
    up4, down4 = hop(up3[:8], UP), hop(down3[8:], DOWN)
    units = [own, up1, down1, up2, down2, up3, down3, up4, down4]
    offsets = [0, -1, 1, -2, 2, -3, 3, -4, 4]
    halves = [None] * 7 + [0, 1]
    units = units + [hop(u, CORES) for u in units]
    owners = [2 * chip_at(place + o) + core for o in offsets]
    owners = owners + [o ^ 1 for o in owners]
    halves = tuple(halves * 2)
    shift = 4 * shard
    owners = jnp.stack(owners + [shift])

    block_count = residual.shape[2]
    flags = jnp.any(jnp.arange(block_count, dtype=jnp.int32)[None, :] == kept_blocks[0, 0][:, None], axis=0)
    flags = flags.astype(jnp.int32)

    xa, slope = run_pre(owners, halves, tokens, x_other, units)
    hd = None
    for i in range(parts):
        hd = run_hid(owners, halves, dy_own[i], dy_other[i], slope, units, i, hd)

    stored = residual.reshape(8, 32, 128, 128)

    def info_of(distances):
        out = []
        for k in distances:
            g = chip_at(place + k)
            a = jnp.where(g < 4, (g - 2 * shard) & 3, 4 + 2 * (g - 4))
            out += [g, a, a]
        return jnp.stack(out + [shift, core])

    new_res = None
    sums = {}
    for distances in ([4], [3, 5], [2, 6, 1, 7, 0]):
        new_res, own_sum, other_sum = run_grads(info_of(distances), flags, xa, hd, stored, new_res, len(distances))
        for i, k in enumerate(distances):
            sums[k] = own_sum[i].astype(F32) + hop(other_sum[i], CORES).astype(F32)

    up, down = hop(sums[4][:8].astype(BF), UP), hop(sums[4][8:].astype(BF), DOWN)
    s3 = sums[3] + jnp.pad(up.astype(F32), ((0, 8), (0, 0), (0, 0)))
    s5 = sums[5] + jnp.pad(down.astype(F32), ((8, 0), (0, 0), (0, 0)))
    up, down = hop(s3.astype(BF), UP), hop(s5.astype(BF), DOWN)
    for k in (2, 1):
        up, down = hop((sums[k] + up.astype(F32)).astype(BF), UP), hop((sums[8 - k] + down.astype(F32)).astype(BF), DOWN)
    owned = sums[0] + up.astype(F32) + down.astype(F32)
    new_momentum = momentum_decay * momentum + owned[None]
    new_master = master - step_size * new_momentum
    return new_master, new_momentum, new_res.reshape(residual.shape)


def local_plain(tokens, out_grad, master, momentum, residual, kept_blocks):
    whole_in = lax.all_gather(tokens, "mp", axis=1, tiled=True)
    whole_grad = lax.all_gather(out_grad, "mp", axis=1, tiled=True)
    tile = master.shape[-1]
    width = whole_in.shape[1]
    block_count = residual.shape[2]
    half = block_count // 2
    rows = width // tile
    cols = half // rows
    working = lax.all_gather(master.astype(BF), "dp", axis=1, tiled=True)[0]
    first_w = working[:half].reshape(rows, cols, tile, tile).transpose(0, 2, 1, 3).reshape(width, cols * tile)
    second_w = working[half:].reshape(cols, rows, tile, tile).transpose(0, 2, 1, 3).reshape(cols * tile, width)
    pre = jnp.dot(whole_in, first_w, preferred_element_type=F32)
    act_full, pullback = jax.vjp(activation, pre)
    act = act_full.astype(BF)
    act_grad = jnp.dot(whole_grad, second_w.T, preferred_element_type=F32)
    hid = pullback(act_grad)[0].astype(BF)
    first_g = jnp.dot(whole_in.T, hid, preferred_element_type=F32)
    second_g = jnp.dot(act.T, whole_grad, preferred_element_type=F32)
    first_g = first_g.reshape(rows, tile, cols, tile).transpose(0, 2, 1, 3).reshape(half, tile, tile)
    second_g = second_g.reshape(cols, tile, rows, tile).transpose(0, 2, 1, 3).reshape(half, tile, tile)
    grads = jnp.concatenate([first_g, second_g], axis=0) + residual[0, 0].astype(F32)
    flags = jnp.any(jnp.arange(block_count, dtype=jnp.int32)[None, :] == kept_blocks[0, 0][:, None], axis=0)
    flags = flags[:, None, None]
    new_residual = jnp.where(flags, 0.0, grads).astype(BF)[None, None]
    owned = lax.psum_scatter(jnp.where(flags, grads, 0.0), "dp", scatter_dimension=0, tiled=True)
    new_momentum = momentum_decay * momentum + owned[None]
    return master - step_size * new_momentum, new_momentum, new_residual


def solution(mesh):
    ring = mesh.shape["dp"] == 16 and mesh.shape["mp"] == 2
    blocks = P("mp", "dp", None, None)
    left = P("dp", "mp", None, None, None)
    return jax.shard_map(
        local_ring if ring else local_plain,
        mesh=mesh,
        in_specs=(P("dp", "mp"), P("dp", "mp"), blocks, blocks, left, P("dp", "mp", None)),
        out_specs=(blocks, blocks, left),
        check_vma=False,
    )
```

```python
import functools

import jax
import jax.numpy as jnp
from jax import lax
from jax.experimental import pallas as pl
from jax.experimental.pallas import tpu as pltpu
from jax.sharding import PartitionSpec as P

momentum_decay = 0.9
step_size = 0.01
BF = jnp.bfloat16
F32 = jnp.float32
ANY = pl.BlockSpec(memory_space=pl.ANY)
HBM = pltpu.HBM
GELU_S = 0.7978845608028654
GELU_C = 0.044715


def activation(values):
    return jax.nn.gelu(values, approximate=True)


def in_hbm(array):
    return pltpu.with_memory_space_constraint(array, HBM)


def gelu_and_slope(v):
    sq = v * v
    t = jnp.tanh(v * (GELU_S + (GELU_S * GELU_C) * sq))
    half = 0.5 + 0.5 * t
    act = v * half
    slope = half + act * (1.0 - t) * (GELU_S + (3.0 * GELU_S * GELU_C) * sq)
    return act, slope


def place_kernel(halves, owners, *refs):
    n = len(halves)
    srcs, (w1, w2, sem) = refs[:n], refs[-3:]
    shift = owners[n]

    def copies(s, first):
        owner, half = owners[s], halves[s]
        if first:
            row = pl.multiple_of(((owner - shift) & 7) * 128, 128)
            return pltpu.make_async_copy(srcs[s], w1.at[pl.ds(8 * half, 8), pl.ds(row, 128)], sem.at[s])
        row = pl.multiple_of((owner - 8) * 256 + 128 * half, 128)
        return pltpu.make_async_copy(srcs[s], w2.at[:, pl.ds(row, 128)], sem.at[s])

    for act in ("start", "wait"):
        for s in range(n):
            for first in (True, False):

                @pl.when((owners[s] < 8) if first else (owners[s] >= 8))
                def _(s=s, first=first):
                    getattr(copies(s, first), act)()


def pre_kernel(x_own, *refs):
    *x_other, w1, act_ref, slope_ref = refs
    w = jnp.concatenate([w1[0], w1[1]], axis=1)
    half = w.shape[0] // 2
    size = x_other[0].shape[0]
    for i, part in enumerate(x_other):
        r = i * size
        pre = jnp.dot(x_own[r : r + size, :], w[:half], preferred_element_type=F32)
        pre += jnp.dot(part[...], w[half:], preferred_element_type=F32)
        act, slope = gelu_and_slope(pre)
        act_ref[r : r + size, :] = act.astype(BF)
        slope_ref[r : r + size, :] = slope


def hid_kernel(shift_ref, dy_own, dy_other, w2, slope_ref, *refs):
    hid = refs[-1]
    shift = shift_ref[0]
    w = jnp.concatenate([w2[(c + shift) & 7] for c in range(8)], axis=1)
    half = w.shape[1] // 2
    dims = (((1,), (1,)), ((), ()))
    g = lax.dot_general(dy_own[...], w[:, :half], dims, preferred_element_type=F32)
    g += lax.dot_general(dy_other[...], w[:, half:], dims, preferred_element_type=F32)
    hid[...] = (g * slope_ref[...]).astype(BF)


def grad_kernel(info, flags, x_own, x_first, x_second, x_third, act_ref, hid_ref, dy_own, dy_first, dy_second, res_ref, *refs):
    new_res, mine, other, grad = refs[-4:]
    group, h = pl.program_id(0), pl.program_id(1)
    g, a = info[2 * group], info[2 * group + 1]
    first = g < 4
    shift, core = info[info.shape[0] - 2], info[info.shape[0] - 1]
    dims = (((0,), (0,)), ((), ()))
    dot = functools.partial(lax.dot_general, dimension_numbers=dims, preferred_element_type=F32)

    @pl.when(first & (a < 2))
    def _():
        grad[...] = dot(x_own[...], hid_ref[...])

    @pl.when(first & (a >= 2))
    def _():
        size = x_first.shape[0]
        parts = enumerate((x_first, x_second, x_third))
        grad[...] = sum(dot(part[...], hid_ref[i * size : (i + 1) * size, :]) for i, part in parts)

    @pl.when(jnp.logical_not(first))
    def _():
        size = dy_first.shape[0]
        grad[:, :512] = dot(act_ref[...], dy_own[...])
        grad[:, 512:] = dot(act_ref[:size, :], dy_first[...]) + dot(act_ref[size:, :], dy_second[...])

    for i in range(2):
        for j in range(8):
            slot = jnp.where(first, 8 * h + j, 8 * i + ((j + shift) & 7))
            target = jnp.where(first, i, h)
            flat = 16 * target + slot
            kept = flags[32 * g + flat] != 0
            v = grad[128 * i : 128 * i + 128, 128 * j : 128 * j + 128] + res_ref[0, flat].astype(F32)
            new_res[0, flat] = jnp.where(kept, 0.0, v).astype(BF)
            send = jnp.where(kept, v, 0.0).astype(BF)

            @pl.when(target == core)
            def _(send=send, slot=slot):
                mine[0, slot] = send

            @pl.when(target != core)
            def _(send=send, slot=slot):
                other[0, slot] = send


def run_place(owners, halves, units, weights):
    operands = [owners, *[in_hbm(u) for u in units]]
    alias = {}
    if weights is not None:
        alias = {len(operands): 0, len(operands) + 1: 1}
        operands += [in_hbm(w) for w in weights]
    return pl.pallas_call(
        functools.partial(place_kernel, halves),
        grid_spec=pltpu.PrefetchScalarGridSpec(
            num_scalar_prefetch=1,
            grid=(1,),
            in_specs=[ANY] * (len(operands) - 1),
            out_specs=[ANY, ANY],
            scratch_shapes=[pltpu.SemaphoreType.DMA((len(units),))],
        ),
        out_shape=[HBM((16, 1024, 128), BF), HBM((8, 2048, 128), BF)],
        input_output_aliases=alias,
        compiler_params=pltpu.CompilerParams(vmem_limit_bytes=2**20),
        cost_estimate=pl.CostEstimate(flops=0, bytes_accessed=len(units) * 2**19, transcendentals=0),
        name="place",
    )(*operands)


def run_pre(x_own, x_other, w1):
    rows = x_own.shape[0]
    full = [pl.BlockSpec(t.shape, lambda i: (0, 0)) for t in (x_own, *x_other)]
    column = pl.BlockSpec((rows, 256), lambda i: (0, i))
    return pl.pallas_call(
        pre_kernel,
        grid=(8,),
        in_specs=[*full, pl.BlockSpec((2, 1024, 128), lambda i: (i, 0, 0))],
        out_specs=[column, column],
        out_shape=[HBM((rows, 2048), BF), HBM((rows, 2048), F32)],
        compiler_params=pltpu.CompilerParams(vmem_limit_bytes=24 * 2**20),
        cost_estimate=pl.CostEstimate(flops=4 * rows * 1024 * 2048, bytes_accessed=26_000_000, transcendentals=rows * 2048),
        name="pre_act",
    )(in_hbm(x_own), *x_other, in_hbm(w1))


def run_hid(shift, dy_own, dy_other, w2, slope, row_block, hid=None):
    rows = dy_other.shape[0]
    column = pl.BlockSpec((rows, 256), lambda i, *_: (row_block, i))
    operands = [shift, in_hbm(dy_own), dy_other, in_hbm(w2), in_hbm(slope)]
    specs = [
        pl.BlockSpec((rows, 512), lambda i, *_: (row_block, 0)),
        pl.BlockSpec((rows, 512), lambda i, *_: (0, 0)),
        pl.BlockSpec((8, 256, 128), lambda i, *_: (0, i, 0)),
        column,
    ]
    alias = {}
    if hid is not None:
        alias = {len(operands): 0}
        operands.append(in_hbm(hid))
        specs.append(ANY)
    return pl.pallas_call(
        hid_kernel,
        grid_spec=pltpu.PrefetchScalarGridSpec(num_scalar_prefetch=1, grid=(8,), in_specs=specs, out_specs=column),
        out_shape=HBM(slope.shape, BF),
        input_output_aliases=alias,
        compiler_params=pltpu.CompilerParams(vmem_limit_bytes=18 * 2**20),
        cost_estimate=pl.CostEstimate(flops=3 * rows * 1024 * 2048, bytes_accessed=15_000_000, transcendentals=0),
        name="hid_grad",
    )(*operands)


def run_grads(info, flags, x_own, x_other, act, hid, dy_own, dy_other, residual, new_res, count):
    rows = act.shape[0]
    block = lambda size: pl.BlockSpec((1, size, 128, 128), lambda i, h, info, *_: (info[2 * i], 0, 0, 0))
    local_block = pl.BlockSpec((1, 16, 128, 128), lambda i, h, *_: (i, 0, 0, 0))
    whole = lambda t: pl.BlockSpec(t.shape, lambda i, h, *_: (0, 0))
    is_first = lambda i, info: info[2 * i] < 4
    held = [in_hbm(t) for t in (act, hid, dy_own)]
    operands = [info, flags, in_hbm(x_own), *x_other, *held, *dy_other, in_hbm(residual)]
    specs = [
        *[
            pl.BlockSpec((t.shape[0], 256), lambda i, h, info, *_: (0, jnp.where(is_first(i, info), info[2 * i + 1] & 1, 0)))
            for t in (x_own, *x_other)
        ],
        pl.BlockSpec((rows, 256), lambda i, h, info, *_: (0, jnp.where(is_first(i, info), 0, info[2 * i + 1] + h))),
        pl.BlockSpec((rows, 1024), lambda i, h, info, *_: (0, jnp.where(is_first(i, info), h, 0))),
        whole(dy_own),
        whole(dy_other[0]),
        whole(dy_other[1]),
        block(32),
    ]
    alias = {}
    if new_res is not None:
        alias = {len(operands): 0}
        operands.append(in_hbm(new_res))
        specs.append(ANY)
    sent = HBM((count, 16, 128, 128), BF)
    return pl.pallas_call(
        grad_kernel,
        grid_spec=pltpu.PrefetchScalarGridSpec(
            num_scalar_prefetch=2,
            grid=(count, 2),
            in_specs=specs,
            out_specs=[block(32), local_block, local_block],
            scratch_shapes=[pltpu.VMEM((256, 1024), F32)],
        ),
        out_shape=[HBM(residual.shape, BF), sent, sent],
        input_output_aliases=alias,
        compiler_params=pltpu.CompilerParams(vmem_limit_bytes=30 * 2**20),
        cost_estimate=pl.CostEstimate(flops=3 * rows * 1024 * 512 * count, bytes_accessed=10_000_000 * count, transcendentals=0),
        name="grad_blocks",
    )(*operands)


def chip_at(place):
    place = place % 8
    if isinstance(place, int):
        return 2 * place if place < 4 else 2 * (7 - place) + 1
    return jnp.where(place < 4, 2 * place, 2 * (7 - place) + 1)


def ring_pairs(step):
    return [(2 * chip_at(p) + c, 2 * chip_at(p + step) + c) for p in range(8) for c in range(2)]


UP, DOWN = ring_pairs(1), ring_pairs(-1)
CORES = [(i, i ^ 1) for i in range(16)]
PAIR = [(0, 1), (1, 0)]


def hop(array, pairs):
    return lax.ppermute(array, "dp", pairs)


def local_ring(tokens, out_grad, master, momentum, residual, kept_blocks):
    mine = lax.axis_index("dp").astype(jnp.int32)
    shard = lax.axis_index("mp").astype(jnp.int32)
    core = mine & 1
    chip = mine >> 1
    place = jnp.where((chip & 1) == 0, chip >> 1, 7 - (chip >> 1))
    rows = tokens.shape[0]

    parts = 2
    size = rows // parts
    dy_own = [out_grad[i * size : (i + 1) * size] for i in range(parts)]
    third = rows // 3
    x_other = [lax.ppermute(t, "mp", PAIR) for t in (tokens[:third], tokens[third : 2 * third], tokens[2 * third :])]
    dy_other = [lax.ppermute(t, "mp", PAIR) for t in dy_own]

    shift = 4 * shard
    own = [master[0, :8].astype(BF), master[0, 8:].astype(BF)]
    up, down = list(own), list(own)
    weights = None
    for k in range(1, 5):
        if k > 1:
            part = k - 2
            x_other[part], *both = lax.optimization_barrier((x_other[part], *up, *down))
            up, down = both[: len(up)], both[len(up) :]
        up = [hop(u, UP) for u in (up if k < 4 else up[:1])]
        down = [hop(u, DOWN) for u in (down if k < 4 else down[1:])]
        if weights is not None:
            *both, weights[0], weights[1] = lax.optimization_barrier((*up, *down, *weights))
            up, down = both[: len(up)], both[len(up) :]
        halves = [0, 1] if k == 4 else [0, 1, 0, 1]
        units = up + down
        owners = [2 * chip_at(place - k) + core] * len(up) + [2 * chip_at(place + k) + core] * len(down)
        if k == 1:
            units, halves, owners = own + units, [0, 1] + halves, [mine, mine] + owners
        units = units + [hop(u, CORES) for u in units]
        owners = jnp.stack(owners + [o ^ 1 for o in owners] + [shift])
        weights = list(run_place(owners, tuple(halves * 2), units, weights))

    block_count = residual.shape[2]
    flags = jnp.any(jnp.arange(block_count, dtype=jnp.int32)[None, :] == kept_blocks[0, 0][:, None], axis=0)
    flags = flags.astype(jnp.int32)

    x_other[2], dy_other[0] = lax.optimization_barrier((x_other[2], dy_other[0]))
    act, slope = run_pre(tokens, x_other, weights[0])
    hid = None
    for i in range(parts):
        hid = run_hid(shift[None], out_grad, dy_other[i], weights[1], slope, i, hid)

    stored = residual.reshape(8, 32, 128, 128)

    def info_of(distances):
        out = []
        for k in distances:
            g = chip_at(place + k)
            a = jnp.where(g < 4, (g - 2 * shard) & 3, 2 * (g - 4))
            out += [g, a]
        return jnp.stack(out + [shift, core])

    new_res, sums, up, down = None, {}, {}, {}

    def add_up(distances):
        nonlocal new_res
        new_res, own_sum, other_sum = run_grads(
            info_of(distances), flags, tokens, x_other, act, hid, out_grad, dy_other, stored, new_res, len(distances)
        )
        other_sum = hop(other_sum, CORES)
        for i, k in enumerate(distances):
            for h in range(2):
                part = slice(8 * h, 8 * h + 8)
                sums[k, h] = own_sum[i, part].astype(F32) + other_sum[i, part].astype(F32)

    def send(k):
        nonlocal flags
        ups = {(k, h): sums[k, h] + (up[k + 1, h].astype(F32) if (k + 1, h) in up else 0.0) for h in range(2) if k < 4 or h == 0}
        downs = {(k, h): sums[8 - k, h] + (down[k + 1, h].astype(F32) if (k + 1, h) in down else 0.0) for h in range(2) if k < 4 or h == 1}
        ups, downs = [{key: t.astype(BF) for key, t in part.items()} for part in (ups, downs)]
        flags, ups, downs = lax.optimization_barrier((flags, ups, downs))
        up.update({key: hop(t, UP) for key, t in ups.items()})
        down.update({key: hop(t, DOWN) for key, t in downs.items()})

    add_up([4])
    add_up([3, 5])
    send(4)
    add_up([2, 6])
    send(3)
    add_up([1, 7, 0])
    send(2)
    send(1)
    owned = jnp.concatenate([sums[0, h] + up[1, h].astype(F32) + down[1, h].astype(F32) for h in range(2)], axis=0)
    new_momentum = momentum_decay * momentum + owned[None]
    new_master = master - step_size * new_momentum
    return new_master, new_momentum, new_res.reshape(residual.shape)


def local_plain(tokens, out_grad, master, momentum, residual, kept_blocks):
    whole_in = lax.all_gather(tokens, "mp", axis=1, tiled=True)
    whole_grad = lax.all_gather(out_grad, "mp", axis=1, tiled=True)
    tile = master.shape[-1]
    width = whole_in.shape[1]
    block_count = residual.shape[2]
    half = block_count // 2
    rows = width // tile
    cols = half // rows
    working = lax.all_gather(master.astype(BF), "dp", axis=1, tiled=True)[0]
    first_w = working[:half].reshape(rows, cols, tile, tile).transpose(0, 2, 1, 3).reshape(width, cols * tile)
    second_w = working[half:].reshape(cols, rows, tile, tile).transpose(0, 2, 1, 3).reshape(cols * tile, width)
    pre = jnp.dot(whole_in, first_w, preferred_element_type=F32)
    act_full, pullback = jax.vjp(activation, pre)
    act = act_full.astype(BF)
    act_grad = jnp.dot(whole_grad, second_w.T, preferred_element_type=F32)
    hid = pullback(act_grad)[0].astype(BF)
    first_g = jnp.dot(whole_in.T, hid, preferred_element_type=F32)
    second_g = jnp.dot(act.T, whole_grad, preferred_element_type=F32)
    first_g = first_g.reshape(rows, tile, cols, tile).transpose(0, 2, 1, 3).reshape(half, tile, tile)
    second_g = second_g.reshape(cols, tile, rows, tile).transpose(0, 2, 1, 3).reshape(half, tile, tile)
    grads = jnp.concatenate([first_g, second_g], axis=0) + residual[0, 0].astype(F32)
    flags = jnp.any(jnp.arange(block_count, dtype=jnp.int32)[None, :] == kept_blocks[0, 0][:, None], axis=0)
    flags = flags[:, None, None]
    new_residual = jnp.where(flags, 0.0, grads).astype(BF)[None, None]
    owned = lax.psum_scatter(jnp.where(flags, grads, 0.0), "dp", scatter_dimension=0, tiled=True)
    new_momentum = momentum_decay * momentum + owned[None]
    return master - step_size * new_momentum, new_momentum, new_residual


def solution(mesh):
    ring = mesh.shape["dp"] == 16 and mesh.shape["mp"] == 2
    blocks = P("mp", "dp", None, None)
    left = P("dp", "mp", None, None, None)
    return jax.shard_map(
        local_ring if ring else local_plain,
        mesh=mesh,
        in_specs=(P("dp", "mp"), P("dp", "mp"), blocks, blocks, left, P("dp", "mp", None)),
        out_specs=(blocks, blocks, left),
        check_vma=False,
    )
```

```python
import functools

import jax
import jax.numpy as jnp
from jax import lax
from jax.experimental import pallas as pl
from jax.experimental.pallas import tpu as pltpu
from jax.sharding import PartitionSpec as P

momentum_decay = 0.9
step_size = 0.01
BF = jnp.bfloat16
F32 = jnp.float32
ANY = pl.BlockSpec(memory_space=pl.ANY)
HBM = pltpu.HBM
GELU_S = 0.7978845608028654
GELU_C = 0.044715


def activation(values):
    return jax.nn.gelu(values, approximate=True)


def in_hbm(array):
    return pltpu.with_memory_space_constraint(array, HBM)


def gelu_and_slope(v):
    sq = v * v
    t = jnp.tanh(v * (GELU_S + (GELU_S * GELU_C) * sq))
    half = 0.5 + 0.5 * t
    act = v * half
    slope = half + act * (1.0 - t) * (GELU_S + (3.0 * GELU_S * GELU_C) * sq)
    return act, slope


def load_weight(halves, first, owners, srcs, dst, sem):
    shift = owners[len(halves)]
    for s, half in enumerate(halves):
        owner = owners[s]

        @pl.when((owner < 8) if first else (owner >= 8))
        def _(s=s, half=half, owner=owner):
            if first:
                row = pl.multiple_of(((owner - shift) & 7) * 128, 128)
                place = dst.at[pl.ds(8 * half, 8), pl.ds(row, 128)]
            else:
                row = pl.multiple_of((owner - 8) * 256 + 128 * half, 128)
                place = dst.at[:, pl.ds(row, 128)]
            pltpu.make_async_copy(srcs[s], place, sem).start()


def pre_kernel(halves, owners, x_own, *refs):
    units, (*x_other, act_t, x_t, slope_ref, w1, sem) = refs[: len(halves)], refs[len(halves) :]
    step = pl.program_id(0)
    size = x_other[0].shape[0]

    @pl.when(step == 0)
    def _():
        load_weight(halves, True, owners, units, w1, sem)

    for s in range(4):

        @pl.when(step == s)
        def _(s=s):
            lanes = slice(256 * (s % 2), 256 * (s % 2) + 256)
            if s < 2:
                x_t[...] = x_own[:, lanes].T
            else:
                for i, part in enumerate(x_other):
                    x_t[:, i * size : (i + 1) * size] = part[:size, lanes].T

    @pl.when(step == 0)
    def _():
        pltpu.make_async_copy(w1, w1, sem).wait()

    w = jnp.concatenate([w1[2 * step], w1[2 * step + 1]], axis=1)
    half = w.shape[0] // 2
    for r in range(0, x_own.shape[0], 256):
        i, o = r // size, r % size
        pre = jnp.dot(x_own[r : r + 256, :], w[:half], preferred_element_type=F32)
        pre += jnp.dot(x_other[i][o : o + 256, :], w[half:], preferred_element_type=F32)
        act, slope = gelu_and_slope(pre)
        act_t[:, r : r + 256] = act.astype(BF).T
        slope_ref[r : r + 256, :] = slope


def hid_first_kernel(halves, owners, dy_own, dy_other, slope_ref, *refs):
    units, (hid, w2_t, w2, sem) = refs[: len(halves)], refs[len(halves) :]
    step = pl.program_id(0)
    shift = owners[len(halves)]

    @pl.when(step == 0)
    def _():
        load_weight(halves, False, owners, units, w2, sem)
        pltpu.make_async_copy(w2, w2, sem).wait()

    row = pl.multiple_of(256 * step, 256)
    for c in range(8):
        w2_t[128 * c : 128 * c + 128, :] = w2[(c + shift) & 7, pl.ds(row, 256), :].T
    hid_block(dy_own, dy_other, w2_t, slope_ref, hid)


def hid_block(dy_own, dy_other, w2_t, slope_ref, hid):
    half = w2_t.shape[0] // 2
    skip = dy_other.shape[0] - dy_own.shape[0]
    for r in range(0, dy_own.shape[0], 256):
        rows = slice(r, r + 256)
        g = jnp.dot(dy_own[rows, :], w2_t[:half, :], preferred_element_type=F32)
        g += jnp.dot(dy_other[r + skip : r + skip + 256, :], w2_t[half:, :], preferred_element_type=F32)
        hid[rows, :] = (g * slope_ref[rows, :]).astype(BF)


def hid_second_kernel(dy_own, dy_other, slope_ref, w2_t, _, hid):
    hid_block(dy_own, dy_other, w2_t, slope_ref, hid)


def grad_kernel(info, flags, x_t, act_t, hid_ref, dy_own, dy_first, dy_second, res_ref, *refs):
    new_res, mine, other = refs[-3:]
    group, h, n = pl.program_id(0), pl.program_id(1), pl.program_id(2)
    g = info[2 * group]
    shift, core = info[info.shape[0] - 2], info[info.shape[0] - 1]
    dot = functools.partial(jnp.dot, preferred_element_type=F32)

    def finish(value, flat):
        kept = flags[32 * g + flat] != 0
        value = value + res_ref[0, flat].astype(F32)
        new_res[0, flat] = jnp.where(kept, 0.0, value).astype(BF)
        return jnp.where(kept, value, 0.0).astype(BF)

    @pl.when(g < 4)
    def _():
        grad = dot(x_t[...], hid_ref[...])
        for out, row in ((mine, core), (other, 1 - core)):
            for j in range(2):
                lanes = slice(128 * j, 128 * j + 128)
                slot = 8 * h + 2 * n + j
                out[0, slot] = finish(jnp.where(row == 0, grad[:128, lanes], grad[128:, lanes]), 16 * row + slot)

    def second(grad, out):
        for i in range(2):
            for j in range(2):
                slot = 8 * i + ((2 * n + j + shift) & 7)
                out[0, slot] = finish(grad[128 * i : 128 * i + 128, 128 * j : 128 * j + 128], 16 * h + slot)

    for out, here in ((mine, h == core), (other, h != core)):

        @pl.when((g >= 4) & here & (n < 2))
        def _(out=out):
            second(dot(act_t[...], dy_own[...]), out)

        @pl.when((g >= 4) & here & (n >= 2))
        def _(out=out):
            size = dy_second.shape[0]
            second(dot(act_t[:, :size], dy_first[dy_first.shape[0] - size :, :]) + dot(act_t[:, size:], dy_second[...]), out)


def run_pre(owners, halves, x_own, x_other, units):
    rows = x_own.shape[0]
    whole = lambda t: pl.BlockSpec(t.shape, lambda i, *_: (0, 0))
    return pl.pallas_call(
        functools.partial(pre_kernel, halves),
        grid_spec=pltpu.PrefetchScalarGridSpec(
            num_scalar_prefetch=1,
            grid=(8,),
            in_specs=[whole(x_own)] + [ANY] * len(units) + [whole(t) for t in x_other],
            out_specs=[
                pl.BlockSpec((256, rows), lambda i, *_: (i, 0)),
                pl.BlockSpec((256, rows), lambda i, *_: (jnp.minimum(i, 3), 0)),
                pl.BlockSpec((rows, 256), lambda i, *_: (0, i)),
            ],
            scratch_shapes=[pltpu.VMEM((16, 1024, 128), BF), pltpu.SemaphoreType.DMA],
        ),
        out_shape=[HBM((2048, rows), BF), HBM((1024, rows), BF), HBM((rows, 2048), F32)],
        compiler_params=pltpu.CompilerParams(vmem_limit_bytes=30 * 2**20),
        cost_estimate=pl.CostEstimate(flops=5 * rows * 1024 * 2048, bytes_accessed=26_000_000, transcendentals=rows * 2048),
        name="pre_act",
    )(owners, in_hbm(x_own), *[in_hbm(u) for u in units], *x_other)


def run_hid_first(owners, halves, dy_own, dy_other, slope, units):
    rows = slope.shape[0] // 2
    column = pl.BlockSpec((rows, 256), lambda i, *_: (0, i))
    part = pl.BlockSpec((rows, 512), lambda i, *_: (0, 0))
    both = pl.BlockSpec(dy_other.shape, lambda i, *_: (0, 0))
    return pl.pallas_call(
        functools.partial(hid_first_kernel, halves),
        grid_spec=pltpu.PrefetchScalarGridSpec(
            num_scalar_prefetch=1,
            grid=(8,),
            in_specs=[part, both, column] + [ANY] * len(units),
            out_specs=[column, pl.BlockSpec((1024, 256), lambda i, *_: (0, i))],
            scratch_shapes=[pltpu.VMEM((8, 2048, 128), BF), pltpu.SemaphoreType.DMA],
        ),
        out_shape=[HBM(slope.shape, BF), HBM((1024, 2048), BF)],
        compiler_params=pltpu.CompilerParams(vmem_limit_bytes=24 * 2**20),
        cost_estimate=pl.CostEstimate(flops=4 * rows * 1024 * 2048, bytes_accessed=18_000_000, transcendentals=0),
        name="hid_first",
    )(owners, in_hbm(dy_own), dy_other, in_hbm(slope), *[in_hbm(u) for u in units])


def run_hid_second(dy_own, dy_other, slope, w2_t, hid):
    rows = dy_other.shape[0]
    column = pl.BlockSpec((rows, 256), lambda i: (1, i))
    return pl.pallas_call(
        hid_second_kernel,
        grid=(8,),
        in_specs=[
            pl.BlockSpec((rows, 512), lambda i: (1, 0)),
            pl.BlockSpec((rows, 512), lambda i: (0, 0)),
            column,
            pl.BlockSpec((1024, 256), lambda i: (0, i)),
            ANY,
        ],
        out_specs=column,
        out_shape=HBM(slope.shape, BF),
        input_output_aliases={4: 0},
        compiler_params=pltpu.CompilerParams(vmem_limit_bytes=20 * 2**20),
        cost_estimate=pl.CostEstimate(flops=3 * rows * 1024 * 2048, bytes_accessed=15_000_000, transcendentals=0),
        name="hid_second",
    )(in_hbm(dy_own), dy_other, in_hbm(slope), in_hbm(w2_t), in_hbm(hid))


def run_grads(info, flags, x_t, act_t, hid, dy_own, dy_other, residual, new_res, count):
    rows = hid.shape[0]
    block = pl.BlockSpec((1, 32, 128, 128), lambda i, h, n, info, *_: (info[2 * i], 0, 0, 0))
    local_block = pl.BlockSpec((1, 16, 128, 128), lambda i, h, n, *_: (i, 0, 0, 0))

    def spec(shape, first, index):
        def at(i, h, n, info, *_):
            return tuple(jnp.where((info[2 * i] < 4) == first, t, 0) for t in index(info[2 * i + 1], h, n))

        return pl.BlockSpec(shape, at)

    held = [in_hbm(t) for t in (x_t, act_t, hid, dy_own)]
    operands = [info, flags, *held, *dy_other, in_hbm(residual)]
    specs = [
        spec((256, rows), True, lambda a, h, n: (a, 0)),
        spec((256, rows), False, lambda a, h, n: (a + h, 0)),
        spec((rows, 256), True, lambda a, h, n: (0, 4 * h + n)),
        spec((rows, 256), False, lambda a, h, n: (0, jnp.minimum(n, 1))),
        *[spec((t.shape[0], 256), False, lambda a, h, n: (0, jnp.maximum(n - 2, 0))) for t in dy_other],
        block,
    ]
    alias = {}
    if new_res is not None:
        alias = {len(operands): 0}
        operands.append(in_hbm(new_res))
        specs.append(ANY)
    sent = HBM((count, 16, 128, 128), BF)
    return pl.pallas_call(
        grad_kernel,
        grid_spec=pltpu.PrefetchScalarGridSpec(
            num_scalar_prefetch=2,
            grid=(count, 2, 4),
            in_specs=specs,
            out_specs=[block, local_block, local_block],
        ),
        out_shape=[HBM(residual.shape, BF), sent, sent],
        input_output_aliases=alias,
        compiler_params=pltpu.CompilerParams(vmem_limit_bytes=24 * 2**20),
        cost_estimate=pl.CostEstimate(flops=3 * rows * 1024 * 512 * count, bytes_accessed=10_000_000 * count, transcendentals=0),
        name="grad_blocks",
    )(*operands)


def chip_at(place):
    place = place % 8
    if isinstance(place, int):
        return 2 * place if place < 4 else 2 * (7 - place) + 1
    return jnp.where(place < 4, 2 * place, 2 * (7 - place) + 1)


def ring_pairs(step):
    return [(2 * chip_at(p) + c, 2 * chip_at(p + step) + c) for p in range(8) for c in range(2)]


UP, DOWN = ring_pairs(1), ring_pairs(-1)
CORES = [(i, i ^ 1) for i in range(16)]
PAIR = [(0, 1), (1, 0)]


def hop(array, pairs):
    return lax.ppermute(array, "dp", pairs)


def local_ring(tokens, out_grad, master, momentum, residual, kept_blocks):
    mine = lax.axis_index("dp").astype(jnp.int32)
    shard = lax.axis_index("mp").astype(jnp.int32)
    core = mine & 1
    chip = mine >> 1
    place = jnp.where((chip & 1) == 0, chip >> 1, 7 - (chip >> 1))
    rows = tokens.shape[0]

    third, half = rows // 3, rows // 2
    swap = lambda t: lax.ppermute(t, "mp", PAIR)
    x_other = [swap(tokens[:third]), swap(tokens[third : 2 * third])]
    x_other.append(swap(jnp.concatenate([tokens[2 * third :], out_grad[:half]], axis=0)))
    dy_late = swap(out_grad[half:])

    shift = 4 * shard
    own = [master[0, :8].astype(BF), master[0, 8:].astype(BF)]
    up, down = list(own), list(own)
    units, halves, owners = list(own), [0, 1], [mine, mine]
    for k in range(1, 5):
        if 1 < k < 4:
            part = k - 2
            x_other[part], *both = lax.optimization_barrier((x_other[part], *up, *down))
            up, down = both[: len(up)], both[len(up) :]
        up = [hop(u, UP) for u in (up if k < 4 else up[:1])]
        down = [hop(u, DOWN) for u in (down if k < 4 else down[1:])]
        halves += [0, 1] if k == 4 else [0, 1, 0, 1]
        units += up + down
        owners += [2 * chip_at(place - k) + core] * len(up) + [2 * chip_at(place + k) + core] * len(down)
    units = units + [hop(u, CORES) for u in units]
    halves = tuple(halves * 2)
    owners = jnp.stack(owners + [o ^ 1 for o in owners] + [shift])

    block_count = residual.shape[2]
    flags = jnp.any(jnp.arange(block_count, dtype=jnp.int32)[None, :] == kept_blocks[0, 0][:, None], axis=0)
    flags = flags.astype(jnp.int32)

    act_t, x_t, slope = run_pre(owners, halves, tokens, x_other, units)
    hid, w2_t = run_hid_first(owners, halves, out_grad, x_other[2], slope, units)
    hid = run_hid_second(out_grad, dy_late, slope, w2_t, hid)
    dy_other = [x_other[2], dy_late]

    stored = residual.reshape(8, 32, 128, 128)

    def info_of(distances):
        out = []
        for k in distances:
            g = chip_at(place + k)
            a = jnp.where(g < 4, (g - 2 * shard) & 3, 2 * (g - 4))
            out += [g, a]
        return jnp.stack(out + [shift, core])

    new_res, sums, up, down = None, {}, {}, {}

    def add_up(distances):
        nonlocal new_res
        new_res, own_sum, other_sum = run_grads(
            info_of(distances), flags, x_t, act_t, hid, out_grad, dy_other, stored, new_res, len(distances)
        )
        other_sum = hop(other_sum, CORES)
        for i, k in enumerate(distances):
            for h in range(2):
                part = slice(8 * h, 8 * h + 8)
                sums[k, h] = own_sum[i, part].astype(F32) + other_sum[i, part].astype(F32)

    def send(k):
        nonlocal flags
        ups = {(k, h): sums[k, h] + (up[k + 1, h].astype(F32) if (k + 1, h) in up else 0.0) for h in range(2) if k < 4 or h == 0}
        downs = {(k, h): sums[8 - k, h] + (down[k + 1, h].astype(F32) if (k + 1, h) in down else 0.0) for h in range(2) if k < 4 or h == 1}
        ups, downs = [{key: t.astype(BF) for key, t in part.items()} for part in (ups, downs)]
        flags, ups, downs = lax.optimization_barrier((flags, ups, downs))
        up.update({key: hop(t, UP) for key, t in ups.items()})
        down.update({key: hop(t, DOWN) for key, t in downs.items()})

    add_up([4])
    add_up([3, 5])
    send(4)
    add_up([2, 6])
    send(3)
    add_up([1, 7, 0])
    send(2)
    send(1)
    owned = jnp.concatenate([sums[0, h] + up[1, h].astype(F32) + down[1, h].astype(F32) for h in range(2)], axis=0)
    new_momentum = momentum_decay * momentum + owned[None]
    new_master = master - step_size * new_momentum
    return new_master, new_momentum, new_res.reshape(residual.shape)


def local_plain(tokens, out_grad, master, momentum, residual, kept_blocks):
    whole_in = lax.all_gather(tokens, "mp", axis=1, tiled=True)
    whole_grad = lax.all_gather(out_grad, "mp", axis=1, tiled=True)
    tile = master.shape[-1]
    width = whole_in.shape[1]
    block_count = residual.shape[2]
    half = block_count // 2
    rows = width // tile
    cols = half // rows
    working = lax.all_gather(master.astype(BF), "dp", axis=1, tiled=True)[0]
    first_w = working[:half].reshape(rows, cols, tile, tile).transpose(0, 2, 1, 3).reshape(width, cols * tile)
    second_w = working[half:].reshape(cols, rows, tile, tile).transpose(0, 2, 1, 3).reshape(cols * tile, width)
    pre = jnp.dot(whole_in, first_w, preferred_element_type=F32)
    act_full, pullback = jax.vjp(activation, pre)
    act = act_full.astype(BF)
    act_grad = jnp.dot(whole_grad, second_w.T, preferred_element_type=F32)
    hid = pullback(act_grad)[0].astype(BF)
    first_g = jnp.dot(whole_in.T, hid, preferred_element_type=F32)
    second_g = jnp.dot(act.T, whole_grad, preferred_element_type=F32)
    first_g = first_g.reshape(rows, tile, cols, tile).transpose(0, 2, 1, 3).reshape(half, tile, tile)
    second_g = second_g.reshape(cols, tile, rows, tile).transpose(0, 2, 1, 3).reshape(half, tile, tile)
    grads = jnp.concatenate([first_g, second_g], axis=0) + residual[0, 0].astype(F32)
    flags = jnp.any(jnp.arange(block_count, dtype=jnp.int32)[None, :] == kept_blocks[0, 0][:, None], axis=0)
    flags = flags[:, None, None]
    new_residual = jnp.where(flags, 0.0, grads).astype(BF)[None, None]
    owned = lax.psum_scatter(jnp.where(flags, grads, 0.0), "dp", scatter_dimension=0, tiled=True)
    new_momentum = momentum_decay * momentum + owned[None]
    return master - step_size * new_momentum, new_momentum, new_residual


def solution(mesh):
    ring = mesh.shape["dp"] == 16 and mesh.shape["mp"] == 2
    blocks = P("mp", "dp", None, None)
    left = P("dp", "mp", None, None, None)
    return jax.shard_map(
        local_ring if ring else local_plain,
        mesh=mesh,
        in_specs=(P("dp", "mp"), P("dp", "mp"), blocks, blocks, left, P("dp", "mp", None)),
        out_specs=(blocks, blocks, left),
        check_vma=False,
    )
```

```python
import functools

import jax
import jax.numpy as jnp
from jax import lax
from jax.experimental import pallas as pl
from jax.experimental.pallas import tpu as pltpu
from jax.sharding import PartitionSpec as P

momentum_decay = 0.9
step_size = 0.01
BF = jnp.bfloat16
F32 = jnp.float32
ANY = pl.BlockSpec(memory_space=pl.ANY)
HBM = pltpu.HBM
GELU_S = 0.7978845608028654
GELU_C = 0.044715


def activation(values):
    return jax.nn.gelu(values, approximate=True)


def in_hbm(array):
    return pltpu.with_memory_space_constraint(array, HBM)


def gelu_and_slope(v):
    sq = v * v
    t = jnp.tanh(v * (GELU_S + (GELU_S * GELU_C) * sq))
    half = 0.5 + 0.5 * t
    act = v * half
    slope = half + act * (1.0 - t) * (GELU_S + (3.0 * GELU_S * GELU_C) * sq)
    return act, slope


def load_weight(halves, first, owners, srcs, dst, sem):
    shift = owners[len(halves)]
    for s, half in enumerate(halves):
        owner = owners[s]

        @pl.when((owner < 8) if first else (owner >= 8))
        def _(s=s, half=half, owner=owner):
            if first:
                row = pl.multiple_of(((owner - shift) & 7) * 128, 128)
                slots = pl.ds(0, 16) if half is None else pl.ds(8 * half, 8)
                pltpu.make_async_copy(srcs[s], dst.at[slots, pl.ds(row, 128)], sem).start()
                return
            for i in (0, 1) if half is None else (half,):
                row = pl.multiple_of((owner - 8) * 256 + 128 * i, 128)
                src = srcs[s].at[pl.ds(8 * i, 8)] if half is None else srcs[s]
                pltpu.make_async_copy(src, dst.at[:, pl.ds(row, 128)], sem).start()


def pre_kernel(halves, owners, x_own, *refs):
    units, (*x_other, act_t, x_t, slope_ref, w1, sem) = refs[: len(halves)], refs[len(halves) :]
    step = pl.program_id(0)
    size = x_other[0].shape[0]

    @pl.when(step == 0)
    def _():
        load_weight(halves, True, owners, units, w1, sem)

    for s in range(4):

        @pl.when(step == s)
        def _(s=s):
            lanes = slice(256 * (s % 2), 256 * (s % 2) + 256)
            if s < 2:
                x_t[...] = x_own[:, lanes].T
            else:
                x_t[:, :size] = x_other[0][:, lanes].T
                x_t[:, size:] = x_other[1][: x_own.shape[0] - size, lanes].T

    @pl.when(step == 0)
    def _():
        pltpu.make_async_copy(w1, w1, sem).wait()

    w = jnp.concatenate([w1[2 * step], w1[2 * step + 1]], axis=1)
    half = w.shape[0] // 2
    for r in range(0, x_own.shape[0], 256):
        i, o = (0, r) if r < size else (1, r - size)
        pre = jnp.dot(x_own[r : r + 256, :], w[:half], preferred_element_type=F32)
        pre += jnp.dot(x_other[i][o : o + 256, :], w[half:], preferred_element_type=F32)
        act, slope = gelu_and_slope(pre)
        act_t[:, r : r + 256] = act.astype(BF).T
        slope_ref[0, r : r + 256, :] = slope


def hid_first_kernel(halves, owners, dy_own, dy_other, slope_ref, *refs):
    units, (hid, dy, w2_t, w2, sem) = refs[: len(halves)], refs[len(halves) :]
    step = pl.program_id(0)
    shift = owners[len(halves)]

    @pl.when(step == 0)
    def _():
        load_weight(halves, False, owners, units, w2, sem)
        pltpu.make_async_copy(w2, w2, sem).wait()

    row = pl.multiple_of(256 * step, 256)
    for c in range(8):
        w2_t[0, 128 * c : 128 * c + 128, :] = w2[(c + shift) & 7, pl.ds(row, 256), :].T
    hid_block(dy_own, dy_other, w2_t, slope_ref, hid, dy)


def hid_block(dy_own, dy_other, w2_t, slope_ref, hid, dy):
    half = w2_t.shape[1] // 2
    skip = dy_other.shape[0] - dy_own.shape[0]
    g = jnp.dot(dy_own[...], w2_t[0, :half, :], preferred_element_type=F32)
    g += jnp.dot(dy_other[skip:, :], w2_t[0, half:, :], preferred_element_type=F32)
    hid[0] = (g * slope_ref[0]).astype(BF)
    for s in range(4):

        @pl.when(pl.program_id(0) == s)
        def _(s=s):
            lanes = slice(256 * (s % 2), 256 * (s % 2) + 256)
            dy[0] = dy_own[:, lanes] if s < 2 else dy_other[skip:, lanes]


def hid_second_kernel(dy_own, dy_other, slope_ref, w2_t, _, __, hid, dy):
    hid_block(dy_own, dy_other, w2_t, slope_ref, hid, dy)


def grad_kernel(info, flags, x_t, act_t, hid_ref, dy_ref, res_ref, *refs):
    new_res, mine, other = refs[-3:]
    group, h, n = pl.program_id(0), pl.program_id(1), pl.program_id(2)
    g = info[2 * group]
    shift, core = info[info.shape[0] - 2], info[info.shape[0] - 1]
    dot = functools.partial(jnp.dot, preferred_element_type=F32)

    def finish(value, flat):
        kept = flags[32 * g + flat] != 0
        value = value + res_ref[0, flat].astype(F32)
        new_res[0, flat] = jnp.where(kept, 0.0, value).astype(BF)
        return jnp.where(kept, value, 0.0).astype(BF)

    @pl.when(g < 4)
    def _():
        for c in range(2):
            grad = dot(x_t[...], hid_ref[c])
            for out, row in ((mine, core), (other, 1 - core)):
                for j in range(2):
                    lanes = slice(128 * j, 128 * j + 128)
                    slot = 8 * h + 4 * n + 2 * c + j
                    out[0, slot] = finish(jnp.where(row == 0, grad[:128, lanes], grad[128:, lanes]), 16 * row + slot)

    for out, here in ((mine, h == core), (other, h != core)):

        @pl.when((g >= 4) & here)
        def _(out=out):
            for c in range(2):
                grad = dot(act_t[...], dy_ref[c])
                for i in range(2):
                    for j in range(2):
                        slot = 8 * i + ((4 * n + 2 * c + j + shift) & 7)
                        out[0, slot] = finish(grad[128 * i : 128 * i + 128, 128 * j : 128 * j + 128], 16 * h + slot)


def run_pre(owners, halves, x_own, x_other, units):
    rows = x_own.shape[0]
    whole = lambda t: pl.BlockSpec(t.shape, lambda i, *_: (0, 0))
    return pl.pallas_call(
        functools.partial(pre_kernel, halves),
        grid_spec=pltpu.PrefetchScalarGridSpec(
            num_scalar_prefetch=1,
            grid=(8,),
            in_specs=[whole(x_own)] + [ANY] * len(units) + [whole(t) for t in x_other],
            out_specs=[
                pl.BlockSpec((256, rows), lambda i, *_: (i, 0)),
                pl.BlockSpec((256, rows), lambda i, *_: (jnp.minimum(i, 3), 0)),
                pl.BlockSpec((1, rows, 256), lambda i, *_: (i, 0, 0)),
            ],
            scratch_shapes=[pltpu.VMEM((16, 1024, 128), BF), pltpu.SemaphoreType.DMA],
        ),
        out_shape=[HBM((2048, rows), BF), HBM((1024, rows), BF), HBM((8, rows, 256), F32)],
        compiler_params=pltpu.CompilerParams(vmem_limit_bytes=30 * 2**20),
        cost_estimate=pl.CostEstimate(flops=5 * rows * 1024 * 2048, bytes_accessed=26_000_000, transcendentals=rows * 2048),
        name="pre_act",
    )(owners, in_hbm(x_own), *[in_hbm(u) for u in units], *x_other)


def run_hid_first(owners, halves, dy_own, dy_other, slope, units):
    total = slope.shape[1]
    rows = total // 2
    part = lambda size: pl.BlockSpec((1, rows, 256), lambda i, *_: (jnp.minimum(i, size - 1), 0, 0))
    return pl.pallas_call(
        functools.partial(hid_first_kernel, halves),
        grid_spec=pltpu.PrefetchScalarGridSpec(
            num_scalar_prefetch=1,
            grid=(8,),
            in_specs=[
                pl.BlockSpec((rows, 512), lambda i, *_: (0, 0)),
                pl.BlockSpec(dy_other.shape, lambda i, *_: (0, 0)),
                part(8),
                *[ANY] * len(units),
            ],
            out_specs=[part(8), part(4), pl.BlockSpec((1, 1024, 256), lambda i, *_: (i, 0, 0))],
            scratch_shapes=[pltpu.VMEM((8, 2048, 128), BF), pltpu.SemaphoreType.DMA],
        ),
        out_shape=[HBM((8, total, 256), BF), HBM((4, total, 256), BF), HBM((8, 1024, 256), BF)],
        compiler_params=pltpu.CompilerParams(vmem_limit_bytes=24 * 2**20),
        cost_estimate=pl.CostEstimate(flops=4 * rows * 1024 * 2048, bytes_accessed=18_000_000, transcendentals=0),
        name="hid_first",
    )(owners, in_hbm(dy_own), dy_other, in_hbm(slope), *[in_hbm(u) for u in units])


def run_hid_second(dy_own, dy_other, slope, w2_t, hid, dy):
    rows = dy_other.shape[0]
    part = lambda size: pl.BlockSpec((1, rows, 256), lambda i: (jnp.minimum(i, size - 1), 1, 0))
    return pl.pallas_call(
        hid_second_kernel,
        grid=(8,),
        in_specs=[
            pl.BlockSpec((rows, 512), lambda i: (1, 0)),
            pl.BlockSpec((rows, 512), lambda i: (0, 0)),
            part(8),
            pl.BlockSpec((1, 1024, 256), lambda i: (i, 0, 0)),
            ANY,
            ANY,
        ],
        out_specs=[part(8), part(4)],
        out_shape=[HBM(hid.shape, BF), HBM(dy.shape, BF)],
        input_output_aliases={4: 0, 5: 1},
        compiler_params=pltpu.CompilerParams(vmem_limit_bytes=20 * 2**20),
        cost_estimate=pl.CostEstimate(flops=3 * rows * 1024 * 2048, bytes_accessed=15_000_000, transcendentals=0),
        name="hid_second",
    )(in_hbm(dy_own), dy_other, in_hbm(slope), in_hbm(w2_t), in_hbm(hid), in_hbm(dy))


def run_grads(info, flags, x_t, act_t, hid, dy, residual, new_res, count):
    rows = hid.shape[1]
    block = pl.BlockSpec((1, 32, 128, 128), lambda i, h, n, info, *_: (info[2 * i], 0, 0, 0))
    local_block = pl.BlockSpec((1, 16, 128, 128), lambda i, h, n, *_: (i, 0, 0, 0))

    def spec(shape, first, index):
        def at(i, h, n, info, *_):
            return tuple(jnp.where((info[2 * i] < 4) == first, t, 0) for t in index(info[2 * i + 1], h, n))

        return pl.BlockSpec(shape, at)

    operands = [info, flags, *[in_hbm(t) for t in (x_t, act_t, hid, dy, residual)]]
    specs = [
        spec((256, rows), True, lambda a, h, n: (a, 0)),
        spec((256, rows), False, lambda a, h, n: (a + h, 0)),
        spec((2, rows, 256), True, lambda a, h, n: (2 * h + n, 0, 0)),
        spec((2, rows, 256), False, lambda a, h, n: (n, 0, 0)),
        block,
    ]
    alias = {}
    if new_res is not None:
        alias = {len(operands): 0}
        operands.append(in_hbm(new_res))
        specs.append(ANY)
    sent = HBM((count, 16, 128, 128), BF)
    return pl.pallas_call(
        grad_kernel,
        grid_spec=pltpu.PrefetchScalarGridSpec(
            num_scalar_prefetch=2,
            grid=(count, 2, 2),
            in_specs=specs,
            out_specs=[block, local_block, local_block],
        ),
        out_shape=[HBM(residual.shape, BF), sent, sent],
        input_output_aliases=alias,
        compiler_params=pltpu.CompilerParams(vmem_limit_bytes=24 * 2**20),
        cost_estimate=pl.CostEstimate(flops=3 * rows * 1024 * 512 * count, bytes_accessed=10_000_000 * count, transcendentals=0),
        name="grad_blocks",
    )(*operands)


def chip_at(place):
    place = place % 8
    if isinstance(place, int):
        return 2 * place if place < 4 else 2 * (7 - place) + 1
    return jnp.where(place < 4, 2 * place, 2 * (7 - place) + 1)


def ring_pairs(step):
    return [(2 * chip_at(p) + c, 2 * chip_at(p + step) + c) for p in range(8) for c in range(2)]


UP, DOWN = ring_pairs(1), ring_pairs(-1)
CORES = [(i, i ^ 1) for i in range(16)]
PAIR = [(0, 1), (1, 0)]


def hop(array, pairs):
    return lax.ppermute(array, "dp", pairs)


def local_ring(tokens, out_grad, master, momentum, residual, kept_blocks):
    mine = lax.axis_index("dp").astype(jnp.int32)
    shard = lax.axis_index("mp").astype(jnp.int32)
    core = mine & 1
    chip = mine >> 1
    place = jnp.where((chip & 1) == 0, chip >> 1, 7 - (chip >> 1))
    rows = tokens.shape[0]

    third, half = rows // 3, rows // 2
    swap = lambda t: lax.ppermute(t, "mp", PAIR)
    x_other = [swap(tokens[:third]), swap(jnp.concatenate([tokens[third:], out_grad[:half]], axis=0))]
    dy_late = swap(out_grad[half:])

    shift = 4 * shard
    own = master[0].astype(BF)
    up = down = own
    units, halves, owners = [own], [None], [mine]
    for k in range(1, 5):
        if k == 2:
            x_other[0], up, down = lax.optimization_barrier((x_other[0], up, down))
        if k == 4:
            up, down = up[:8], down[8:]
        up, down = hop(up, UP), hop(down, DOWN)
        halves += [0, 1] if k == 4 else [None, None]
        units += [up, down]
        owners += [2 * chip_at(place - k) + core, 2 * chip_at(place + k) + core]
    units = units + [hop(u, CORES) for u in units]
    halves = tuple(halves * 2)
    owners = jnp.stack(owners + [o ^ 1 for o in owners] + [shift])

    block_count = residual.shape[2]
    flags = jnp.any(jnp.arange(block_count, dtype=jnp.int32)[None, :] == kept_blocks[0, 0][:, None], axis=0)
    flags = flags.astype(jnp.int32)

    act_t, x_t, slope = run_pre(owners, halves, tokens, x_other, units)
    hid, dy, w2_t = run_hid_first(owners, halves, out_grad, x_other[1], slope, units)
    hid, dy = run_hid_second(out_grad, dy_late, slope, w2_t, hid, dy)

    stored = residual.reshape(8, 32, 128, 128)

    def info_of(distances):
        out = []
        for k in distances:
            g = chip_at(place + k)
            a = jnp.where(g < 4, (g - 2 * shard) & 3, 2 * (g - 4))
            out += [g, a]
        return jnp.stack(out + [shift, core])

    new_res, sums, up, down = None, {}, {}, {}

    def add_up(distances):
        nonlocal new_res
        new_res, own_sum, other_sum = run_grads(
            info_of(distances), flags, x_t, act_t, hid, dy, stored, new_res, len(distances)
        )
        other_sum = hop(other_sum, CORES)
        for i, k in enumerate(distances):
            for h in range(2):
                part = slice(8 * h, 8 * h + 8)
                sums[k, h] = own_sum[i, part].astype(F32) + other_sum[i, part].astype(F32)

    def send(k):
        nonlocal flags
        ups = {(k, h): sums[k, h] + (up[k + 1, h].astype(F32) if (k + 1, h) in up else 0.0) for h in range(2) if k < 4 or h == 0}
        downs = {(k, h): sums[8 - k, h] + (down[k + 1, h].astype(F32) if (k + 1, h) in down else 0.0) for h in range(2) if k < 4 or h == 1}
        ups, downs = [{key: t.astype(BF) for key, t in part.items()} for part in (ups, downs)]
        flags, ups, downs = lax.optimization_barrier((flags, ups, downs))
        up.update({key: hop(t, UP) for key, t in ups.items()})
        down.update({key: hop(t, DOWN) for key, t in downs.items()})

    add_up([4])
    add_up([3, 5])
    send(4)
    add_up([2, 6])
    send(3)
    add_up([1, 7, 0])
    send(2)
    send(1)
    owned = jnp.concatenate([sums[0, h] + up[1, h].astype(F32) + down[1, h].astype(F32) for h in range(2)], axis=0)
    new_momentum = momentum_decay * momentum + owned[None]
    new_master = master - step_size * new_momentum
    return new_master, new_momentum, new_res.reshape(residual.shape)


def local_plain(tokens, out_grad, master, momentum, residual, kept_blocks):
    whole_in = lax.all_gather(tokens, "mp", axis=1, tiled=True)
    whole_grad = lax.all_gather(out_grad, "mp", axis=1, tiled=True)
    tile = master.shape[-1]
    width = whole_in.shape[1]
    block_count = residual.shape[2]
    half = block_count // 2
    rows = width // tile
    cols = half // rows
    working = lax.all_gather(master.astype(BF), "dp", axis=1, tiled=True)[0]
    first_w = working[:half].reshape(rows, cols, tile, tile).transpose(0, 2, 1, 3).reshape(width, cols * tile)
    second_w = working[half:].reshape(cols, rows, tile, tile).transpose(0, 2, 1, 3).reshape(cols * tile, width)
    pre = jnp.dot(whole_in, first_w, preferred_element_type=F32)
    act_full, pullback = jax.vjp(activation, pre)
    act = act_full.astype(BF)
    act_grad = jnp.dot(whole_grad, second_w.T, preferred_element_type=F32)
    hid = pullback(act_grad)[0].astype(BF)
    first_g = jnp.dot(whole_in.T, hid, preferred_element_type=F32)
    second_g = jnp.dot(act.T, whole_grad, preferred_element_type=F32)
    first_g = first_g.reshape(rows, tile, cols, tile).transpose(0, 2, 1, 3).reshape(half, tile, tile)
    second_g = second_g.reshape(cols, tile, rows, tile).transpose(0, 2, 1, 3).reshape(half, tile, tile)
    grads = jnp.concatenate([first_g, second_g], axis=0) + residual[0, 0].astype(F32)
    flags = jnp.any(jnp.arange(block_count, dtype=jnp.int32)[None, :] == kept_blocks[0, 0][:, None], axis=0)
    flags = flags[:, None, None]
    new_residual = jnp.where(flags, 0.0, grads).astype(BF)[None, None]
    owned = lax.psum_scatter(jnp.where(flags, grads, 0.0), "dp", scatter_dimension=0, tiled=True)
    new_momentum = momentum_decay * momentum + owned[None]
    return master - step_size * new_momentum, new_momentum, new_residual


def solution(mesh):
    ring = mesh.shape["dp"] == 16 and mesh.shape["mp"] == 2
    blocks = P("mp", "dp", None, None)
    left = P("dp", "mp", None, None, None)
    return jax.shard_map(
        local_ring if ring else local_plain,
        mesh=mesh,
        in_specs=(P("dp", "mp"), P("dp", "mp"), blocks, blocks, left, P("dp", "mp", None)),
        out_specs=(blocks, blocks, left),
        check_vma=False,
    )
```

```python
import functools

import jax
import jax.numpy as jnp
from jax import lax
from jax.experimental import pallas as pl
from jax.experimental.pallas import tpu as pltpu
from jax.sharding import PartitionSpec as P

momentum_decay = 0.9
step_size = 0.01
BF = jnp.bfloat16
F32 = jnp.float32
ANY = pl.BlockSpec(memory_space=pl.ANY)
HBM = pltpu.HBM
VMEM = pltpu.VMEM
GELU_S = 0.7978845608028654
GELU_C = 0.044715


def activation(values):
    return jax.nn.gelu(values, approximate=True)


def in_hbm(array):
    return pltpu.with_memory_space_constraint(array, HBM)


def in_vmem(array):
    return pltpu.with_memory_space_constraint(array, VMEM)


def gelu_and_slope(v):
    sq = v * v
    t = jnp.tanh(v * (GELU_S + (GELU_S * GELU_C) * sq))
    half = 0.5 + 0.5 * t
    act = v * half
    slope = half + act * (1.0 - t) * (GELU_S + (3.0 * GELU_S * GELU_C) * sq)
    return act, slope


def load_weight(halves, first, owners, srcs, dst, sem):
    shift = owners[len(halves)]
    for s, half in enumerate(halves):
        owner = owners[s]

        @pl.when((owner < 8) if first else (owner >= 8))
        def _(s=s, half=half, owner=owner):
            if first:
                row = pl.multiple_of(((owner - shift) & 7) * 128, 128)
                slots = pl.ds(0, 16) if half is None else pl.ds(8 * half, 8)
                pltpu.make_async_copy(srcs[s], dst.at[slots, pl.ds(row, 128)], sem).start()
                return
            for i in (0, 1) if half is None else (half,):
                row = pl.multiple_of((owner - 8) * 256 + 128 * i, 128)
                src = srcs[s].at[pl.ds(8 * i, 8)] if half is None else srcs[s]
                pltpu.make_async_copy(src, dst.at[:, pl.ds(row, 128)], sem).start()


def pre_kernel(halves, owners, x_own, *refs):
    units, (*x_other, act_t, x_t, slope_ref, w1, sem) = refs[: len(halves)], refs[len(halves) :]
    step = pl.program_id(0)
    size = x_other[0].shape[0]

    @pl.when(step == 0)
    def _():
        load_weight(halves, True, owners, units, w1, sem)

    for s in range(4):

        @pl.when(step == s)
        def _(s=s):
            lanes = slice(256 * (s % 2), 256 * (s % 2) + 256)
            if s < 2:
                x_t[...] = x_own[:, lanes].T
            else:
                x_t[:, :size] = x_other[0][:, lanes].T
                x_t[:, size:] = x_other[1][: x_own.shape[0] - size, lanes].T

    @pl.when(step == 0)
    def _():
        pltpu.make_async_copy(w1, w1, sem).wait()

    w = jnp.concatenate([w1[2 * step], w1[2 * step + 1]], axis=1)
    half = w.shape[0] // 2
    for r in range(0, x_own.shape[0], 256):
        i, o = (0, r) if r < size else (1, r - size)
        pre = jnp.dot(x_own[r : r + 256, :], w[:half], preferred_element_type=F32)
        pre += jnp.dot(x_other[i][o : o + 256, :], w[half:], preferred_element_type=F32)
        act, slope = gelu_and_slope(pre)
        act_t[:, r : r + 256] = act.astype(BF).T
        slope_ref[0, r : r + 256, :] = slope


def hid_first_kernel(halves, owners, dy_own, dy_other, slope_ref, *refs):
    units, (hid, dy, w2_t, w2, sem) = refs[: len(halves)], refs[len(halves) :]
    step = pl.program_id(0)
    shift = owners[len(halves)]

    @pl.when(step == 0)
    def _():
        load_weight(halves, False, owners, units, w2, sem)
        pltpu.make_async_copy(w2, w2, sem).wait()

    for j in range(2):
        row = pl.multiple_of(512 * step + 256 * j, 256)
        for c in range(8):
            w2_t[j, 128 * c : 128 * c + 128, :] = w2[(c + shift) & 7, pl.ds(row, 256), :].T
    hid_block(dy_own, dy_other, w2_t, slope_ref, hid, dy)


def hid_block(dy_own, dy_other, w2_t, slope_ref, hid, dy):
    half = w2_t.shape[1] // 2
    skip = dy_other.shape[0] - dy_own.shape[0]
    for j in range(2):
        g = jnp.dot(dy_own[...], w2_t[j, :half, :], preferred_element_type=F32)
        g += jnp.dot(dy_other[skip:, :], w2_t[j, half:, :], preferred_element_type=F32)
        hid[j] = (g * slope_ref[j]).astype(BF)
    for s in range(4):

        @pl.when(pl.program_id(0) == s)
        def _(s=s):
            lanes = slice(256 * (s % 2), 256 * (s % 2) + 256)
            dy[0] = dy_own[:, lanes] if s < 2 else dy_other[skip:, lanes]


def hid_second_kernel(dy_own, dy_other, slope_ref, w2_t, _, __, hid, dy):
    hid_block(dy_own, dy_other, w2_t, slope_ref, hid, dy)


def grad_kernel(info, flags, x_t, act_t, hid_ref, dy_ref, res_ref, *refs):
    new_res, mine, other = refs[-3:]
    group, h = pl.program_id(0), pl.program_id(1)
    g = info[2 * group]
    shift, core = info[info.shape[0] - 2], info[info.shape[0] - 1]
    dot = functools.partial(jnp.dot, preferred_element_type=F32)

    def finish(value, flat):
        kept = flags[32 * g + flat] != 0
        value = value + res_ref[0, flat].astype(F32)
        new_res[0, flat] = jnp.where(kept, 0.0, value).astype(BF)
        return jnp.where(kept, value, 0.0).astype(BF)

    @pl.when(g < 4)
    def _():
        for c in range(4):
            grad = dot(x_t[...], hid_ref[c])
            for out, row in ((mine, core), (other, 1 - core)):
                for j in range(2):
                    lanes = slice(128 * j, 128 * j + 128)
                    slot = 8 * h + 2 * c + j
                    out[0, slot] = finish(jnp.where(row == 0, grad[:128, lanes], grad[128:, lanes]), 16 * row + slot)

    for out, here in ((mine, h == core), (other, h != core)):

        @pl.when((g >= 4) & here)
        def _(out=out):
            for c in range(4):
                grad = dot(act_t[...], dy_ref[c])
                for i in range(2):
                    for j in range(2):
                        slot = 8 * i + ((2 * c + j + shift) & 7)
                        out[0, slot] = finish(grad[128 * i : 128 * i + 128, 128 * j : 128 * j + 128], 16 * h + slot)


def run_pre(owners, halves, x_own, x_other, units):
    rows = x_own.shape[0]
    whole = lambda t: pl.BlockSpec(t.shape, lambda i, *_: (0, 0))
    return pl.pallas_call(
        functools.partial(pre_kernel, halves),
        grid_spec=pltpu.PrefetchScalarGridSpec(
            num_scalar_prefetch=1,
            grid=(8,),
            in_specs=[whole(x_own)] + [ANY] * len(units) + [whole(t) for t in x_other],
            out_specs=[
                pl.BlockSpec((256, rows), lambda i, *_: (i, 0)),
                pl.BlockSpec((256, rows), lambda i, *_: (jnp.minimum(i, 3), 0)),
                pl.BlockSpec((1, rows, 256), lambda i, *_: (i, 0, 0)),
            ],
            scratch_shapes=[pltpu.VMEM((16, 1024, 128), BF), pltpu.SemaphoreType.DMA],
        ),
        out_shape=[VMEM((2048, rows), BF), VMEM((1024, rows), BF), HBM((8, rows, 256), F32)],
        compiler_params=pltpu.CompilerParams(vmem_limit_bytes=24 * 2**20),
        cost_estimate=pl.CostEstimate(flops=5 * rows * 1024 * 2048, bytes_accessed=26_000_000, transcendentals=rows * 2048),
        name="pre_act",
    )(owners, in_hbm(x_own), *[in_hbm(u) for u in units], *x_other)


def run_hid_first(owners, halves, dy_own, dy_other, slope, units):
    total = slope.shape[1]
    rows = total // 2
    part = lambda size: pl.BlockSpec((size, rows, 256), lambda i, *_: (i, 0, 0))
    return pl.pallas_call(
        functools.partial(hid_first_kernel, halves),
        grid_spec=pltpu.PrefetchScalarGridSpec(
            num_scalar_prefetch=1,
            grid=(4,),
            in_specs=[
                pl.BlockSpec((rows, 512), lambda i, *_: (0, 0)),
                pl.BlockSpec(dy_other.shape, lambda i, *_: (0, 0)),
                part(2),
                *[ANY] * len(units),
            ],
            out_specs=[part(2), part(1), pl.BlockSpec((2, 1024, 256), lambda i, *_: (i, 0, 0))],
            scratch_shapes=[pltpu.VMEM((8, 2048, 128), BF), pltpu.SemaphoreType.DMA],
        ),
        out_shape=[VMEM((8, total, 256), BF), VMEM((4, total, 256), BF), VMEM((8, 1024, 256), BF)],
        compiler_params=pltpu.CompilerParams(vmem_limit_bytes=22 * 2**20),
        cost_estimate=pl.CostEstimate(flops=4 * rows * 1024 * 2048, bytes_accessed=18_000_000, transcendentals=0),
        name="hid_first",
    )(owners, in_hbm(dy_own), dy_other, in_hbm(slope), *[in_hbm(u) for u in units])


def run_hid_second(dy_own, dy_other, slope, w2_t, hid, dy):
    rows = dy_other.shape[0]
    part = lambda size: pl.BlockSpec((size, rows, 256), lambda i: (i, 1, 0))
    return pl.pallas_call(
        hid_second_kernel,
        grid=(4,),
        in_specs=[
            pl.BlockSpec((rows, 512), lambda i: (1, 0)),
            pl.BlockSpec((rows, 512), lambda i: (0, 0)),
            part(2),
            pl.BlockSpec((2, 1024, 256), lambda i: (i, 0, 0)),
            ANY,
            ANY,
        ],
        out_specs=[part(2), part(1)],
        out_shape=[VMEM(hid.shape, BF), VMEM(dy.shape, BF)],
        input_output_aliases={4: 0, 5: 1},
        compiler_params=pltpu.CompilerParams(vmem_limit_bytes=18 * 2**20),
        cost_estimate=pl.CostEstimate(flops=3 * rows * 1024 * 2048, bytes_accessed=15_000_000, transcendentals=0),
        name="hid_second",
    )(in_hbm(dy_own), dy_other, in_hbm(slope), in_vmem(w2_t), in_vmem(hid), in_vmem(dy))


def run_grads(info, flags, x_t, act_t, hid, dy, residual, new_res, count, pin):
    rows = hid.shape[1]
    block = pl.BlockSpec((1, 32, 128, 128), lambda i, h, info, *_: (info[2 * i], 0, 0, 0))
    local_block = pl.BlockSpec((1, 16, 128, 128), lambda i, h, *_: (i, 0, 0, 0))

    def spec(shape, first, index):
        def at(i, h, info, *_):
            return tuple(jnp.where((info[2 * i] < 4) == first, t, 0) for t in index(info[2 * i + 1], h))

        return pl.BlockSpec(shape, at)

    operands = [info, flags, *[pin(t) for t in (x_t, act_t, hid, dy)], in_hbm(residual)]
    specs = [
        spec((256, rows), True, lambda a, h: (a, 0)),
        spec((256, rows), False, lambda a, h: (a + h, 0)),
        spec((4, rows, 256), True, lambda a, h: (h, 0, 0)),
        spec((4, rows, 256), False, lambda a, h: (0, 0, 0)),
        block,
    ]
    alias = {}
    if new_res is not None:
        alias = {len(operands): 0}
        operands.append(in_hbm(new_res))
        specs.append(ANY)
    sent = HBM((count, 16, 128, 128), BF)
    return pl.pallas_call(
        grad_kernel,
        grid_spec=pltpu.PrefetchScalarGridSpec(
            num_scalar_prefetch=2,
            grid=(count, 2),
            in_specs=specs,
            out_specs=[block, local_block, local_block],
        ),
        out_shape=[HBM(residual.shape, BF), sent, sent],
        input_output_aliases=alias,
        compiler_params=pltpu.CompilerParams(vmem_limit_bytes=28 * 2**20),
        cost_estimate=pl.CostEstimate(flops=3 * rows * 1024 * 512 * count, bytes_accessed=10_000_000 * count, transcendentals=0),
        name="grad_blocks",
    )(*operands)


def chip_at(place):
    place = place % 8
    if isinstance(place, int):
        return 2 * place if place < 4 else 2 * (7 - place) + 1
    return jnp.where(place < 4, 2 * place, 2 * (7 - place) + 1)


def ring_pairs(step):
    return [(2 * chip_at(p) + c, 2 * chip_at(p + step) + c) for p in range(8) for c in range(2)]


UP, DOWN = ring_pairs(1), ring_pairs(-1)
CORES = [(i, i ^ 1) for i in range(16)]
PAIR = [(0, 1), (1, 0)]


def hop(array, pairs):
    return lax.ppermute(array, "dp", pairs)


def local_ring(tokens, out_grad, master, momentum, residual, kept_blocks):
    mine = lax.axis_index("dp").astype(jnp.int32)
    shard = lax.axis_index("mp").astype(jnp.int32)
    core = mine & 1
    chip = mine >> 1
    place = jnp.where((chip & 1) == 0, chip >> 1, 7 - (chip >> 1))
    rows = tokens.shape[0]

    third, half = rows // 3, rows // 2
    swap = lambda t: lax.ppermute(t, "mp", PAIR)
    x_other = [swap(tokens[:third]), swap(jnp.concatenate([tokens[third:], out_grad[:half]], axis=0))]
    dy_late = swap(out_grad[half:])

    shift = 4 * shard
    own = master[0].astype(BF)
    up = down = own
    units, halves, owners = [own], [None], [mine]
    for k in range(1, 5):
        if k == 2:
            x_other[0], up, down = lax.optimization_barrier((x_other[0], up, down))
        if k == 4:
            up, down = up[:8], down[8:]
        up, down = hop(up, UP), hop(down, DOWN)
        halves += [0, 1] if k == 4 else [None, None]
        units += [up, down]
        owners += [2 * chip_at(place - k) + core, 2 * chip_at(place + k) + core]
    units = units + [hop(u, CORES) for u in units]
    halves = tuple(halves * 2)
    owners = jnp.stack(owners + [o ^ 1 for o in owners] + [shift])

    block_count = residual.shape[2]
    flags = jnp.any(jnp.arange(block_count, dtype=jnp.int32)[None, :] == kept_blocks[0, 0][:, None], axis=0)
    flags = flags.astype(jnp.int32)

    act_t, x_t, slope = run_pre(owners, halves, tokens, x_other, units)
    hid, dy, w2_t = run_hid_first(owners, halves, out_grad, x_other[1], slope, units)
    hid, dy = run_hid_second(out_grad, dy_late, slope, w2_t, hid, dy)

    stored = residual.reshape(8, 32, 128, 128)

    def info_of(distances):
        out = []
        for k in distances:
            g = chip_at(place + k)
            a = jnp.where(g < 4, (g - 2 * shard) & 3, 2 * (g - 4))
            out += [g, a]
        return jnp.stack(out + [shift, core])

    new_res, sums, up, down = None, {}, {}, {}

    def add_up(distances, pin):
        nonlocal new_res
        new_res, own_sum, other_sum = run_grads(
            info_of(distances), flags, x_t, act_t, hid, dy, stored, new_res, len(distances), pin
        )
        other_sum = hop(other_sum, CORES)
        for i, k in enumerate(distances):
            for h in range(2):
                part = slice(8 * h, 8 * h + 8)
                sums[k, h] = own_sum[i, part].astype(F32) + other_sum[i, part].astype(F32)

    def send(k):
        nonlocal flags
        ups = {(k, h): sums[k, h] + (up[k + 1, h].astype(F32) if (k + 1, h) in up else 0.0) for h in range(2) if k < 4 or h == 0}
        downs = {(k, h): sums[8 - k, h] + (down[k + 1, h].astype(F32) if (k + 1, h) in down else 0.0) for h in range(2) if k < 4 or h == 1}
        ups, downs = [{key: t.astype(BF) for key, t in part.items()} for part in (ups, downs)]
        flags, ups, downs = lax.optimization_barrier((flags, ups, downs))
        up.update({key: hop(t, UP) for key, t in ups.items()})
        down.update({key: hop(t, DOWN) for key, t in downs.items()})

    add_up([4], in_vmem)
    add_up([3, 5], in_vmem)
    send(4)
    add_up([2, 6], in_hbm)
    send(3)
    add_up([1, 7, 0], in_hbm)
    send(2)
    send(1)
    owned = jnp.concatenate([sums[0, h] + up[1, h].astype(F32) + down[1, h].astype(F32) for h in range(2)], axis=0)
    new_momentum = momentum_decay * momentum + owned[None]
    new_master = master - step_size * new_momentum
    return new_master, new_momentum, new_res.reshape(residual.shape)


def local_plain(tokens, out_grad, master, momentum, residual, kept_blocks):
    whole_in = lax.all_gather(tokens, "mp", axis=1, tiled=True)
    whole_grad = lax.all_gather(out_grad, "mp", axis=1, tiled=True)
    tile = master.shape[-1]
    width = whole_in.shape[1]
    block_count = residual.shape[2]
    half = block_count // 2
    rows = width // tile
    cols = half // rows
    working = lax.all_gather(master.astype(BF), "dp", axis=1, tiled=True)[0]
    first_w = working[:half].reshape(rows, cols, tile, tile).transpose(0, 2, 1, 3).reshape(width, cols * tile)
    second_w = working[half:].reshape(cols, rows, tile, tile).transpose(0, 2, 1, 3).reshape(cols * tile, width)
    pre = jnp.dot(whole_in, first_w, preferred_element_type=F32)
    act_full, pullback = jax.vjp(activation, pre)
    act = act_full.astype(BF)
    act_grad = jnp.dot(whole_grad, second_w.T, preferred_element_type=F32)
    hid = pullback(act_grad)[0].astype(BF)
    first_g = jnp.dot(whole_in.T, hid, preferred_element_type=F32)
    second_g = jnp.dot(act.T, whole_grad, preferred_element_type=F32)
    first_g = first_g.reshape(rows, tile, cols, tile).transpose(0, 2, 1, 3).reshape(half, tile, tile)
    second_g = second_g.reshape(cols, tile, rows, tile).transpose(0, 2, 1, 3).reshape(half, tile, tile)
    grads = jnp.concatenate([first_g, second_g], axis=0) + residual[0, 0].astype(F32)
    flags = jnp.any(jnp.arange(block_count, dtype=jnp.int32)[None, :] == kept_blocks[0, 0][:, None], axis=0)
    flags = flags[:, None, None]
    new_residual = jnp.where(flags, 0.0, grads).astype(BF)[None, None]
    owned = lax.psum_scatter(jnp.where(flags, grads, 0.0), "dp", scatter_dimension=0, tiled=True)
    new_momentum = momentum_decay * momentum + owned[None]
    return master - step_size * new_momentum, new_momentum, new_residual


def solution(mesh):
    ring = mesh.shape["dp"] == 16 and mesh.shape["mp"] == 2
    blocks = P("mp", "dp", None, None)
    left = P("dp", "mp", None, None, None)
    return jax.shard_map(
        local_ring if ring else local_plain,
        mesh=mesh,
        in_specs=(P("dp", "mp"), P("dp", "mp"), blocks, blocks, left, P("dp", "mp", None)),
        out_specs=(blocks, blocks, left),
        check_vma=False,
    )
```

```python
import functools

import jax
import jax.numpy as jnp
from jax import lax
from jax.experimental import pallas as pl
from jax.experimental.pallas import tpu as pltpu
from jax.sharding import PartitionSpec as P

momentum_decay = 0.9
step_size = 0.01
BF = jnp.bfloat16
F32 = jnp.float32
ANY = pl.BlockSpec(memory_space=pl.ANY)
HBM = pltpu.HBM
VMEM = pltpu.VMEM
GELU_S = 0.7978845608028654
GELU_C = 0.044715


def activation(values):
    return jax.nn.gelu(values, approximate=True)


def in_hbm(array):
    return pltpu.with_memory_space_constraint(array, HBM)


def in_vmem(array):
    return pltpu.with_memory_space_constraint(array, VMEM)


def gelu_and_slope(v):
    sq = v * v
    t = jnp.tanh(v * (GELU_S + (GELU_S * GELU_C) * sq))
    half = 0.5 + 0.5 * t
    act = v * half
    slope = half + act * (1.0 - t) * (GELU_S + (3.0 * GELU_S * GELU_C) * sq)
    return act, slope


def load_weight(halves, first, owners, srcs, dst, sem):
    shift = owners[len(halves)]
    for s, half in enumerate(halves):
        owner = owners[s]

        @pl.when((owner < 8) if first else (owner >= 8))
        def _(s=s, half=half, owner=owner):
            if first:
                row = pl.multiple_of(((owner - shift) & 7) * 128, 128)
                slots = pl.ds(0, 16) if half is None else pl.ds(8 * half, 8)
                pltpu.make_async_copy(srcs[s], dst.at[slots, pl.ds(row, 128)], sem).start()
                return
            for i in (0, 1) if half is None else (half,):
                row = pl.multiple_of((owner - 8) * 256 + 128 * i, 128)
                src = srcs[s].at[pl.ds(8 * i, 8)] if half is None else srcs[s]
                pltpu.make_async_copy(src, dst.at[:, pl.ds(row, 128)], sem).start()


def pre_kernel(halves, owners, x_own, *refs):
    units, (x_first, x_second, left_t, slope_ref, w1, sem) = refs[: len(halves)], refs[len(halves) :]
    step = pl.program_id(0)
    rows, size = x_own.shape[0], x_first.shape[0]

    @pl.when(step == 0)
    def _():
        load_weight(halves, True, owners, units, w1, sem)

    for s in range(4):

        @pl.when(step == s)
        def _(s=s):
            lanes = slice(256 * (s % 2), 256 * (s % 2) + 256)
            if s < 2:
                left_t[...] = x_own[:, lanes].T
            else:
                left_t[:, :size] = x_first[:, lanes].T
                left_t[:, size:] = x_second[: rows - size, lanes].T

    @pl.when(step == 4)
    def _():
        pltpu.make_async_copy(w1, w1, sem).wait()

    @pl.when(step >= 4)
    def _():
        c = 2 * (step - 4)
        w = jnp.concatenate([w1[c], w1[c + 1]], axis=1)
        block = size // 2

        def product(r):
            part, o = (x_first, r) if r < size else (x_second, r - size)
            x = jnp.concatenate([x_own[r : r + block, :], part[o : o + block, :]], axis=1)
            return jnp.dot(x, w, preferred_element_type=F32)

        starts = list(range(0, rows, block))
        ahead = product(starts[0])
        for i, r in enumerate(starts):
            pre = ahead
            if i + 1 < len(starts):
                ahead = product(starts[i + 1])
            act, slope = gelu_and_slope(pre)
            left_t[:, r : r + block] = act.astype(BF).T
            slope_ref[0, r : r + block, :] = slope


def hid_first_kernel(halves, owners, dy_own, dy_other, slope_ref, *refs):
    units, (right, w2_t, w2, sem) = refs[: len(halves)], refs[len(halves) :]
    step = pl.program_id(0)
    shift = owners[len(halves)]

    @pl.when(step == 0)
    def _():
        load_weight(halves, False, owners, units, w2, sem)

    @pl.when(step == 2)
    def _():
        pltpu.make_async_copy(w2, w2, sem).wait()

    @pl.when(step >= 2)
    def _():
        for j in range(2):
            row = pl.multiple_of(512 * (step - 2) + 256 * j, 256)
            for c in range(8):
                w2_t[j, 128 * c : 128 * c + 128, :] = w2[(c + shift) & 7, pl.ds(row, 256), :].T

    hid_block(dy_own, dy_other, w2_t, slope_ref, right)


def hid_block(dy_own, dy_other, w2_t, slope_ref, right):
    step = pl.program_id(0)
    skip = dy_other.shape[0] - dy_own.shape[0]

    @pl.when(step < 2)
    def _():
        for j in range(2):
            lanes = slice(256 * j, 256 * j + 256)
            right[j] = jnp.where(step == 0, dy_own[:, lanes], dy_other[skip:, lanes])

    @pl.when(step >= 2)
    def _():
        dy = jnp.concatenate([dy_own[...], dy_other[skip:, :]], axis=1)
        for j in range(2):
            g = jnp.dot(dy, w2_t[j], preferred_element_type=F32)
            right[j] = (g * slope_ref[j]).astype(BF)


def hid_second_kernel(dy_own, dy_other, slope_ref, w2_t, _, right):
    hid_block(dy_own, dy_other, w2_t, slope_ref, right)


def grad_kernel(info, flags, left_ref, right_ref, res_ref, *refs):
    new_res, mine, other = refs[-3:]
    group, h = pl.program_id(0), pl.program_id(1)
    g = info[2 * group]
    shift, core = info[info.shape[0] - 2], info[info.shape[0] - 1]
    dot = functools.partial(jnp.dot, preferred_element_type=F32)

    def finish(value, flat):
        kept = flags[32 * g + flat] != 0
        value = value + res_ref[0, flat].astype(F32)
        new_res[0, flat] = jnp.where(kept, 0.0, value).astype(BF)
        return jnp.where(kept, value, 0.0).astype(BF)

    @pl.when(g < 4)
    def _():
        for c in range(4):
            grad = dot(left_ref[...], right_ref[c])
            for out, row in ((mine, core), (other, 1 - core)):
                for j in range(2):
                    lanes = slice(128 * j, 128 * j + 128)
                    slot = 8 * h + 2 * c + j
                    out[0, slot] = finish(jnp.where(row == 0, grad[:128, lanes], grad[128:, lanes]), 16 * row + slot)

    for out, here in ((mine, h == core), (other, h != core)):

        @pl.when((g >= 4) & here)
        def _(out=out):
            for c in range(4):
                grad = dot(left_ref[...], right_ref[c])
                for i in range(2):
                    for j in range(2):
                        slot = 8 * i + ((2 * c + j + shift) & 7)
                        out[0, slot] = finish(grad[128 * i : 128 * i + 128, 128 * j : 128 * j + 128], 16 * h + slot)


def run_pre(owners, halves, x_own, x_other, units):
    rows = x_own.shape[0]
    whole = lambda t: pl.BlockSpec(t.shape, lambda i, *_: (0, 0))
    return pl.pallas_call(
        functools.partial(pre_kernel, halves),
        grid_spec=pltpu.PrefetchScalarGridSpec(
            num_scalar_prefetch=1,
            grid=(12,),
            in_specs=[whole(x_own)] + [ANY] * len(units) + [whole(t) for t in x_other],
            out_specs=[
                pl.BlockSpec((256, rows), lambda i, *_: (i, 0)),
                pl.BlockSpec((1, rows, 256), lambda i, *_: (jnp.maximum(i - 4, 0), 0, 0)),
            ],
            scratch_shapes=[pltpu.VMEM((16, 1024, 128), BF), pltpu.SemaphoreType.DMA],
        ),
        out_shape=[VMEM((3072, rows), BF), HBM((8, rows, 256), F32)],
        compiler_params=pltpu.CompilerParams(vmem_limit_bytes=24 * 2**20),
        cost_estimate=pl.CostEstimate(flops=5 * rows * 1024 * 2048, bytes_accessed=26_000_000, transcendentals=rows * 2048),
        name="pre_act",
    )(owners, in_hbm(x_own), *[in_hbm(u) for u in units], *x_other)


def run_hid_first(owners, halves, dy_own, dy_other, slope, units):
    total = slope.shape[1]
    rows = total // 2
    later = lambda i: jnp.maximum(i - 2, 0)
    return pl.pallas_call(
        functools.partial(hid_first_kernel, halves),
        grid_spec=pltpu.PrefetchScalarGridSpec(
            num_scalar_prefetch=1,
            grid=(6,),
            in_specs=[
                pl.BlockSpec((rows, 512), lambda i, *_: (0, 0)),
                pl.BlockSpec(dy_other.shape, lambda i, *_: (0, 0)),
                pl.BlockSpec((2, rows, 256), lambda i, *_: (later(i), 0, 0)),
                *[ANY] * len(units),
            ],
            out_specs=[
                pl.BlockSpec((2, rows, 256), lambda i, *_: (jnp.where(i < 2, i + 4, i - 2), 0, 0)),
                pl.BlockSpec((2, 1024, 256), lambda i, *_: (later(i), 0, 0)),
            ],
            scratch_shapes=[pltpu.VMEM((8, 2048, 128), BF), pltpu.SemaphoreType.DMA],
        ),
        out_shape=[VMEM((12, total, 256), BF), VMEM((8, 1024, 256), BF)],
        compiler_params=pltpu.CompilerParams(vmem_limit_bytes=22 * 2**20),
        cost_estimate=pl.CostEstimate(flops=4 * rows * 1024 * 2048, bytes_accessed=18_000_000, transcendentals=0),
        name="hid_first",
    )(owners, in_hbm(dy_own), in_hbm(dy_other), in_hbm(slope), *[in_hbm(u) for u in units])


def run_hid_second(dy_own, dy_other, slope, w2_t, right):
    rows = dy_other.shape[0]
    later = lambda i: jnp.maximum(i - 2, 0)
    return pl.pallas_call(
        hid_second_kernel,
        grid=(6,),
        in_specs=[
            pl.BlockSpec((rows, 512), lambda i: (1, 0)),
            pl.BlockSpec((rows, 512), lambda i: (0, 0)),
            pl.BlockSpec((2, rows, 256), lambda i: (later(i), 1, 0)),
            pl.BlockSpec((2, 1024, 256), lambda i: (later(i), 0, 0)),
            ANY,
        ],
        out_specs=pl.BlockSpec((2, rows, 256), lambda i: (jnp.where(i < 2, i + 4, i - 2), 1, 0)),
        out_shape=VMEM(right.shape, BF),
        input_output_aliases={4: 0},
        compiler_params=pltpu.CompilerParams(vmem_limit_bytes=18 * 2**20),
        cost_estimate=pl.CostEstimate(flops=3 * rows * 1024 * 2048, bytes_accessed=15_000_000, transcendentals=0),
        name="hid_second",
    )(in_hbm(dy_own), dy_other, in_hbm(slope), in_vmem(w2_t), in_vmem(right))


def run_grads(info, flags, left_t, right, residual, new_res, count, pin):
    rows = right.shape[1]
    block = pl.BlockSpec((1, 32, 128, 128), lambda i, h, info, *_: (info[2 * i], 0, 0, 0))
    local_block = pl.BlockSpec((1, 16, 128, 128), lambda i, h, *_: (i, 0, 0, 0))
    pick = lambda i, info, first, second: jnp.where(info[2 * i] < 4, first, second)
    operands = [info, flags, pin(left_t), pin(right), in_hbm(residual)]
    specs = [
        pl.BlockSpec((256, rows), lambda i, h, info, *_: (pick(i, info, info[2 * i + 1], info[2 * i + 1] + h + 4), 0)),
        pl.BlockSpec((4, rows, 256), lambda i, h, info, *_: (pick(i, info, h, 2), 0, 0)),
        block,
    ]
    alias = {}
    if new_res is not None:
        alias = {len(operands): 0}
        operands.append(in_hbm(new_res))
        specs.append(ANY)
    sent = HBM((count, 16, 128, 128), BF)
    return pl.pallas_call(
        grad_kernel,
        grid_spec=pltpu.PrefetchScalarGridSpec(
            num_scalar_prefetch=2,
            grid=(count, 2),
            in_specs=specs,
            out_specs=[block, local_block, local_block],
        ),
        out_shape=[HBM(residual.shape, BF), sent, sent],
        input_output_aliases=alias,
        compiler_params=pltpu.CompilerParams(vmem_limit_bytes=20 * 2**20),
        cost_estimate=pl.CostEstimate(flops=4 * rows * 1024 * 512 * count, bytes_accessed=10_000_000 * count, transcendentals=0),
        name="grad_blocks",
    )(*operands)


def chip_at(place):
    place = place % 8
    if isinstance(place, int):
        return 2 * place if place < 4 else 2 * (7 - place) + 1
    return jnp.where(place < 4, 2 * place, 2 * (7 - place) + 1)


def ring_pairs(step):
    return [(2 * chip_at(p) + c, 2 * chip_at(p + step) + c) for p in range(8) for c in range(2)]


UP, DOWN = ring_pairs(1), ring_pairs(-1)
CORES = [(i, i ^ 1) for i in range(16)]
PAIR = [(0, 1), (1, 0)]


def hop(array, pairs):
    return lax.ppermute(array, "dp", pairs)


def local_ring(tokens, out_grad, master, momentum, residual, kept_blocks):
    mine = lax.axis_index("dp").astype(jnp.int32)
    shard = lax.axis_index("mp").astype(jnp.int32)
    core = mine & 1
    chip = mine >> 1
    place = jnp.where((chip & 1) == 0, chip >> 1, 7 - (chip >> 1))
    rows = tokens.shape[0]

    half = rows // 2
    swap = lambda t: lax.ppermute(t, "mp", PAIR)
    x_other = [swap(tokens[:half]), swap(jnp.concatenate([tokens[half:], out_grad[:half]], axis=0))]
    dy_late = swap(out_grad[half:])

    shift = 4 * shard
    own = master[0].astype(BF)
    up = down = own
    units, halves, owners = [own], [None], [mine]
    for k in range(1, 5):
        if k == 2:
            x_other[0], up, down = lax.optimization_barrier((x_other[0], up, down))
        if k == 4:
            up, down = up[:8], down[8:]
        up, down = hop(up, UP), hop(down, DOWN)
        halves += [0, 1] if k == 4 else [None, None]
        units += [up, down]
        owners += [2 * chip_at(place - k) + core, 2 * chip_at(place + k) + core]
    units = units + [hop(u, CORES) for u in units]
    halves = tuple(halves * 2)
    owners = jnp.stack(owners + [o ^ 1 for o in owners] + [shift])

    block_count = residual.shape[2]
    flags = jnp.any(jnp.arange(block_count, dtype=jnp.int32)[None, :] == kept_blocks[0, 0][:, None], axis=0)
    flags = flags.astype(jnp.int32)

    left_t, slope = run_pre(owners, halves, tokens, x_other, units)
    right, w2_t = run_hid_first(owners, halves, out_grad, x_other[1], slope, units)
    right = run_hid_second(out_grad, dy_late, slope, w2_t, right)

    stored = residual.reshape(8, 32, 128, 128)

    def info_of(distances):
        out = []
        for k in distances:
            g = chip_at(place + k)
            a = jnp.where(g < 4, (g - 2 * shard) & 3, 2 * (g - 4))
            out += [g, a]
        return jnp.stack(out + [shift, core])

    new_res, sums, up, down = None, {}, {}, {}

    def add_up(distances, pin):
        nonlocal new_res
        new_res, own_sum, other_sum = run_grads(
            info_of(distances), flags, left_t, right, stored, new_res, len(distances), pin
        )
        other_sum = hop(other_sum, CORES)
        for i, k in enumerate(distances):
            for h in range(2):
                part = slice(8 * h, 8 * h + 8)
                sums[k, h] = own_sum[i, part].astype(F32) + other_sum[i, part].astype(F32)

    def send(k):
        nonlocal flags
        ups = {(k, h): sums[k, h] + (up[k + 1, h].astype(F32) if (k + 1, h) in up else 0.0) for h in range(2) if k < 4 or h == 0}
        downs = {(k, h): sums[8 - k, h] + (down[k + 1, h].astype(F32) if (k + 1, h) in down else 0.0) for h in range(2) if k < 4 or h == 1}
        ups, downs = [{key: t.astype(BF) for key, t in part.items()} for part in (ups, downs)]
        flags, ups, downs = lax.optimization_barrier((flags, ups, downs))
        up.update({key: hop(t, UP) for key, t in ups.items()})
        down.update({key: hop(t, DOWN) for key, t in downs.items()})

    add_up([4], in_vmem)
    add_up([3, 5], in_vmem)
    send(4)
    add_up([2], in_hbm)
    add_up([6], in_hbm)
    send(3)
    add_up([1], in_hbm)
    add_up([7], in_hbm)
    send(2)
    add_up([0], in_hbm)
    send(1)
    owned = jnp.concatenate([sums[0, h] + up[1, h].astype(F32) + down[1, h].astype(F32) for h in range(2)], axis=0)
    new_momentum = momentum_decay * momentum + owned[None]
    new_master = master - step_size * new_momentum
    return new_master, new_momentum, new_res.reshape(residual.shape)


def local_plain(tokens, out_grad, master, momentum, residual, kept_blocks):
    whole_in = lax.all_gather(tokens, "mp", axis=1, tiled=True)
    whole_grad = lax.all_gather(out_grad, "mp", axis=1, tiled=True)
    tile = master.shape[-1]
    width = whole_in.shape[1]
    block_count = residual.shape[2]
    half = block_count // 2
    rows = width // tile
    cols = half // rows
    working = lax.all_gather(master.astype(BF), "dp", axis=1, tiled=True)[0]
    first_w = working[:half].reshape(rows, cols, tile, tile).transpose(0, 2, 1, 3).reshape(width, cols * tile)
    second_w = working[half:].reshape(cols, rows, tile, tile).transpose(0, 2, 1, 3).reshape(cols * tile, width)
    pre = jnp.dot(whole_in, first_w, preferred_element_type=F32)
    act_full, pullback = jax.vjp(activation, pre)
    act = act_full.astype(BF)
    act_grad = jnp.dot(whole_grad, second_w.T, preferred_element_type=F32)
    hid = pullback(act_grad)[0].astype(BF)
    first_g = jnp.dot(whole_in.T, hid, preferred_element_type=F32)
    second_g = jnp.dot(act.T, whole_grad, preferred_element_type=F32)
    first_g = first_g.reshape(rows, tile, cols, tile).transpose(0, 2, 1, 3).reshape(half, tile, tile)
    second_g = second_g.reshape(cols, tile, rows, tile).transpose(0, 2, 1, 3).reshape(half, tile, tile)
    grads = jnp.concatenate([first_g, second_g], axis=0) + residual[0, 0].astype(F32)
    flags = jnp.any(jnp.arange(block_count, dtype=jnp.int32)[None, :] == kept_blocks[0, 0][:, None], axis=0)
    flags = flags[:, None, None]
    new_residual = jnp.where(flags, 0.0, grads).astype(BF)[None, None]
    owned = lax.psum_scatter(jnp.where(flags, grads, 0.0), "dp", scatter_dimension=0, tiled=True)
    new_momentum = momentum_decay * momentum + owned[None]
    return master - step_size * new_momentum, new_momentum, new_residual


def solution(mesh):
    ring = mesh.shape["dp"] == 16 and mesh.shape["mp"] == 2
    blocks = P("mp", "dp", None, None)
    left = P("dp", "mp", None, None, None)
    return jax.shard_map(
        local_ring if ring else local_plain,
        mesh=mesh,
        in_specs=(P("dp", "mp"), P("dp", "mp"), blocks, blocks, left, P("dp", "mp", None)),
        out_specs=(blocks, blocks, left),
        check_vma=False,
    )
```

```python
import functools

import jax
import jax.numpy as jnp
from jax import lax
from jax.experimental import pallas as pl
from jax.experimental.pallas import tpu as pltpu
from jax.sharding import PartitionSpec as P

momentum_decay = 0.9
step_size = 0.01
BF = jnp.bfloat16
F32 = jnp.float32
ANY = pl.BlockSpec(memory_space=pl.ANY)
HBM = pltpu.HBM
VMEM = pltpu.VMEM
GELU_S = 0.7978845608028654
GELU_C = 0.044715


def activation(values):
    return jax.nn.gelu(values, approximate=True)


def in_hbm(array):
    return pltpu.with_memory_space_constraint(array, HBM)


def in_vmem(array):
    return pltpu.with_memory_space_constraint(array, VMEM)


def gelu_and_slope(v):
    sq = v * v
    t = jnp.tanh(v * (GELU_S + (GELU_S * GELU_C) * sq))
    half = 0.5 + 0.5 * t
    act = v * half
    slope = half + act * (1.0 - t) * (GELU_S + (3.0 * GELU_S * GELU_C) * sq)
    return act, slope


def load_weight(halves, first, owners, srcs, dst, sem):
    shift = owners[len(halves)]
    for s, half in enumerate(halves):
        owner = owners[s]

        @pl.when((owner < 8) if first else (owner >= 8))
        def _(s=s, half=half, owner=owner):
            if first:
                row = pl.multiple_of(((owner - shift) & 7) * 128, 128)
                slots = pl.ds(0, 16) if half is None else pl.ds(8 * half, 8)
                pltpu.make_async_copy(srcs[s], dst.at[slots, pl.ds(row, 128)], sem).start()
                return
            for i in (0, 1) if half is None else (half,):
                row = pl.multiple_of((owner - 8) * 256 + 128 * i, 128)
                src = srcs[s].at[pl.ds(8 * i, 8)] if half is None else srcs[s]
                pltpu.make_async_copy(src, dst.at[:, pl.ds(row, 128)], sem).start()


def pre_kernel(halves, owners, x_own, *refs):
    units, (x_first, x_second, left_t, slope_ref, w1, sem) = refs[: len(halves)], refs[len(halves) :]
    step = pl.program_id(0)
    rows, size = x_own.shape[0], x_first.shape[0]

    @pl.when(step == 0)
    def _():
        load_weight(halves, True, owners, units, w1, sem)

    for s in range(4):

        @pl.when(step == s)
        def _(s=s):
            lanes = slice(256 * (s % 2), 256 * (s % 2) + 256)
            if s < 2:
                left_t[...] = x_own[:, lanes].T
            else:
                left_t[:, :size] = x_first[:, lanes].T
                left_t[:, size:] = x_second[: rows - size, lanes].T

    @pl.when(step == 4)
    def _():
        pltpu.make_async_copy(w1, w1, sem).wait()

    @pl.when(step >= 4)
    def _():
        c = 2 * (step - 4)
        w = jnp.concatenate([w1[c], w1[c + 1]], axis=1)
        block = size // 2

        def product(r):
            part, o = (x_first, r) if r < size else (x_second, r - size)
            pre = jnp.dot(x_own[r : r + block, :], w[: w.shape[0] // 2], preferred_element_type=F32)
            return pre + jnp.dot(part[o : o + block, :], w[w.shape[0] // 2 :], preferred_element_type=F32)

        starts = list(range(0, rows, block))
        ahead = product(starts[0])
        for i, r in enumerate(starts):
            pre = ahead
            if i + 1 < len(starts):
                ahead = product(starts[i + 1])
            act, slope = gelu_and_slope(pre)
            left_t[:, r : r + block] = act.astype(BF).T
            slope_ref[0, r : r + block, :] = slope


def hid_first_kernel(halves, owners, dy_own, dy_other, slope_ref, *refs):
    units, (right, w2_t, w2, sem) = refs[: len(halves)], refs[len(halves) :]
    step = pl.program_id(0)
    shift = owners[len(halves)]

    @pl.when(step == 0)
    def _():
        load_weight(halves, False, owners, units, w2, sem)

    @pl.when(step == 2)
    def _():
        pltpu.make_async_copy(w2, w2, sem).wait()

    @pl.when(step >= 2)
    def _():
        for j in range(2):
            row = pl.multiple_of(512 * (step - 2) + 256 * j, 256)
            for c in range(8):
                w2_t[j, 128 * c : 128 * c + 128, :] = w2[(c + shift) & 7, pl.ds(row, 256), :].T

    hid_block(dy_own, dy_other, w2_t, slope_ref, right)


def hid_block(dy_own, dy_other, w2_t, slope_ref, right):
    step = pl.program_id(0)
    skip = dy_other.shape[0] - dy_own.shape[0]

    @pl.when(step < 2)
    def _():
        for j in range(2):
            lanes = slice(256 * j, 256 * j + 256)
            right[j] = jnp.where(step == 0, dy_own[:, lanes], dy_other[skip:, lanes])

    @pl.when(step >= 2)
    def _():
        half = w2_t.shape[1] // 2
        for j in range(2):
            g = jnp.dot(dy_own[...], w2_t[j, :half, :], preferred_element_type=F32)
            g += jnp.dot(dy_other[skip:, :], w2_t[j, half:, :], preferred_element_type=F32)
            right[j] = (g * slope_ref[j]).astype(BF)


def hid_second_kernel(dy_own, dy_other, slope_ref, w2_t, _, right):
    hid_block(dy_own, dy_other, w2_t, slope_ref, right)


def grad_kernel(info, flags, left_ref, right_ref, res_ref, *refs):
    new_res, mine, other = refs[-3:]
    group, h = pl.program_id(0), pl.program_id(1)
    g = info[2 * group]
    row = pl.multiple_of(256 * (info[2 * group + 1] + jnp.where(g < 4, 0, h + 4)), 256)
    left = left_ref.at[pl.ds(row, 256)]
    shift, core = info[info.shape[0] - 2], info[info.shape[0] - 1]
    dot = functools.partial(jnp.dot, preferred_element_type=F32)

    def finish(value, flat):
        kept = flags[32 * g + flat] != 0
        value = value + res_ref[0, flat].astype(F32)
        new_res[0, flat] = jnp.where(kept, 0.0, value).astype(BF)
        return jnp.where(kept, value, 0.0).astype(BF)

    @pl.when(g < 4)
    def _():
        for c in range(4):
            grad = dot(left[...], right_ref[4 * h + c])
            for out, row in ((mine, core), (other, 1 - core)):
                for j in range(2):
                    lanes = slice(128 * j, 128 * j + 128)
                    slot = 8 * h + 2 * c + j
                    out[0, slot] = finish(jnp.where(row == 0, grad[:128, lanes], grad[128:, lanes]), 16 * row + slot)

    for out, here in ((mine, h == core), (other, h != core)):

        @pl.when((g >= 4) & here)
        def _(out=out):
            for c in range(4):
                grad = dot(left[...], right_ref[8 + c])
                for i in range(2):
                    for j in range(2):
                        slot = 8 * i + ((2 * c + j + shift) & 7)
                        out[0, slot] = finish(grad[128 * i : 128 * i + 128, 128 * j : 128 * j + 128], 16 * h + slot)


def run_pre(owners, halves, x_own, x_other, units):
    rows = x_own.shape[0]
    whole = lambda t: pl.BlockSpec(t.shape, lambda i, *_: (0, 0))
    return pl.pallas_call(
        functools.partial(pre_kernel, halves),
        grid_spec=pltpu.PrefetchScalarGridSpec(
            num_scalar_prefetch=1,
            grid=(12,),
            in_specs=[whole(x_own)] + [ANY] * len(units) + [whole(t) for t in x_other],
            out_specs=[
                pl.BlockSpec((256, rows), lambda i, *_: (i, 0)),
                pl.BlockSpec((1, rows, 256), lambda i, *_: (jnp.maximum(i - 4, 0), 0, 0)),
            ],
            scratch_shapes=[pltpu.VMEM((16, 1024, 128), BF), pltpu.SemaphoreType.DMA],
        ),
        out_shape=[VMEM((3072, rows), BF), HBM((8, rows, 256), F32)],
        compiler_params=pltpu.CompilerParams(vmem_limit_bytes=24 * 2**20),
        cost_estimate=pl.CostEstimate(flops=5 * rows * 1024 * 2048, bytes_accessed=26_000_000, transcendentals=rows * 2048),
        name="pre_act",
    )(owners, in_hbm(x_own), *[in_hbm(u) for u in units], *x_other)


def run_hid_first(owners, halves, dy_own, dy_other, slope, units):
    total = slope.shape[1]
    rows = total // 2
    later = lambda i: jnp.maximum(i - 2, 0)
    return pl.pallas_call(
        functools.partial(hid_first_kernel, halves),
        grid_spec=pltpu.PrefetchScalarGridSpec(
            num_scalar_prefetch=1,
            grid=(6,),
            in_specs=[
                pl.BlockSpec((rows, 512), lambda i, *_: (0, 0)),
                pl.BlockSpec(dy_other.shape, lambda i, *_: (0, 0)),
                pl.BlockSpec((2, rows, 256), lambda i, *_: (later(i), 0, 0)),
                *[ANY] * len(units),
            ],
            out_specs=[
                pl.BlockSpec((2, rows, 256), lambda i, *_: (jnp.where(i < 2, i + 4, i - 2), 0, 0)),
                pl.BlockSpec((2, 1024, 256), lambda i, *_: (later(i), 0, 0)),
            ],
            scratch_shapes=[pltpu.VMEM((8, 2048, 128), BF), pltpu.SemaphoreType.DMA],
        ),
        out_shape=[VMEM((12, total, 256), BF), VMEM((8, 1024, 256), BF)],
        compiler_params=pltpu.CompilerParams(vmem_limit_bytes=22 * 2**20),
        cost_estimate=pl.CostEstimate(flops=4 * rows * 1024 * 2048, bytes_accessed=18_000_000, transcendentals=0),
        name="hid_first",
    )(owners, in_hbm(dy_own), in_hbm(dy_other), in_hbm(slope), *[in_hbm(u) for u in units])


def run_hid_second(dy_own, dy_other, slope, w2_t, right):
    rows = dy_other.shape[0]
    later = lambda i: jnp.maximum(i - 2, 0)
    return pl.pallas_call(
        hid_second_kernel,
        grid=(6,),
        in_specs=[
            pl.BlockSpec((rows, 512), lambda i: (1, 0)),
            pl.BlockSpec((rows, 512), lambda i: (0, 0)),
            pl.BlockSpec((2, rows, 256), lambda i: (later(i), 1, 0)),
            pl.BlockSpec((2, 1024, 256), lambda i: (later(i), 0, 0)),
            ANY,
        ],
        out_specs=pl.BlockSpec((2, rows, 256), lambda i: (jnp.where(i < 2, i + 4, i - 2), 1, 0)),
        out_shape=VMEM(right.shape, BF),
        input_output_aliases={4: 0},
        compiler_params=pltpu.CompilerParams(vmem_limit_bytes=18 * 2**20),
        cost_estimate=pl.CostEstimate(flops=3 * rows * 1024 * 2048, bytes_accessed=15_000_000, transcendentals=0),
        name="hid_second",
    )(in_hbm(dy_own), dy_other, in_hbm(slope), in_vmem(w2_t), in_vmem(right))


def run_grads(info, flags, left_t, right, residual, new_res, count):
    rows = right.shape[1]
    block = pl.BlockSpec((1, 32, 128, 128), lambda i, h, info, *_: (info[2 * i], 0, 0, 0))
    local_block = pl.BlockSpec((1, 16, 128, 128), lambda i, h, *_: (i, 0, 0, 0))
    operands = [info, flags, in_vmem(left_t), in_vmem(right), in_hbm(residual)]
    specs = [
        pl.BlockSpec(left_t.shape, lambda i, h, *_: (0, 0)),
        pl.BlockSpec(right.shape, lambda i, h, *_: (0, 0, 0)),
        block,
    ]
    alias = {}
    if new_res is not None:
        alias = {len(operands): 0}
        operands.append(in_hbm(new_res))
        specs.append(ANY)
    sent = HBM((count, 16, 128, 128), BF)
    return pl.pallas_call(
        grad_kernel,
        grid_spec=pltpu.PrefetchScalarGridSpec(
            num_scalar_prefetch=2,
            grid=(count, 2),
            in_specs=specs,
            out_specs=[block, local_block, local_block],
        ),
        out_shape=[HBM(residual.shape, BF), sent, sent],
        input_output_aliases=alias,
        compiler_params=pltpu.CompilerParams(vmem_limit_bytes=20 * 2**20),
        cost_estimate=pl.CostEstimate(flops=4 * rows * 1024 * 512 * count, bytes_accessed=10_000_000 * count, transcendentals=0),
        name="grad_blocks",
    )(*operands)


def chip_at(place):
    place = place % 8
    if isinstance(place, int):
        return 2 * place if place < 4 else 2 * (7 - place) + 1
    return jnp.where(place < 4, 2 * place, 2 * (7 - place) + 1)


def ring_pairs(step):
    return [(2 * chip_at(p) + c, 2 * chip_at(p + step) + c) for p in range(8) for c in range(2)]


UP, DOWN = ring_pairs(1), ring_pairs(-1)
CORES = [(i, i ^ 1) for i in range(16)]
PAIR = [(0, 1), (1, 0)]


def hop(array, pairs):
    return lax.ppermute(array, "dp", pairs)


def local_ring(tokens, out_grad, master, momentum, residual, kept_blocks):
    mine = lax.axis_index("dp").astype(jnp.int32)
    shard = lax.axis_index("mp").astype(jnp.int32)
    core = mine & 1
    chip = mine >> 1
    place = jnp.where((chip & 1) == 0, chip >> 1, 7 - (chip >> 1))
    rows = tokens.shape[0]

    half = rows // 2
    swap = lambda t: lax.ppermute(t, "mp", PAIR)
    x_other = [swap(tokens[:half]), swap(jnp.concatenate([tokens[half:], out_grad[:half]], axis=0))]
    dy_late = swap(out_grad[half:])

    shift = 4 * shard
    own = master[0].astype(BF)
    up = down = own
    units, halves, owners = [own], [None], [mine]
    for k in range(1, 5):
        if k == 2:
            x_other[0], up, down = lax.optimization_barrier((x_other[0], up, down))
        if k == 4:
            up, down = up[:8], down[8:]
        up, down = hop(up, UP), hop(down, DOWN)
        halves += [0, 1] if k == 4 else [None, None]
        units += [up, down]
        owners += [2 * chip_at(place - k) + core, 2 * chip_at(place + k) + core]
    units = units + [hop(u, CORES) for u in units]
    halves = tuple(halves * 2)
    owners = jnp.stack(owners + [o ^ 1 for o in owners] + [shift])

    block_count = residual.shape[2]
    flags = jnp.any(jnp.arange(block_count, dtype=jnp.int32)[None, :] == kept_blocks[0, 0][:, None], axis=0)
    flags = flags.astype(jnp.int32)

    left_t, slope = run_pre(owners, halves, tokens, x_other, units)
    right, w2_t = run_hid_first(owners, halves, out_grad, x_other[1], slope, units)
    right = run_hid_second(out_grad, dy_late, slope, w2_t, right)

    stored = residual.reshape(8, 32, 128, 128)

    def info_of(distances):
        out = []
        for k in distances:
            g = chip_at(place + k)
            a = jnp.where(g < 4, (g - 2 * shard) & 3, 2 * (g - 4))
            out += [g, a]
        return jnp.stack(out + [shift, core])

    new_res, sums, up, down = None, {}, {}, {}

    def add_up(distances):
        nonlocal new_res
        new_res, own_sum, other_sum = run_grads(
            info_of(distances), flags, left_t, right, stored, new_res, len(distances)
        )
        other_sum = hop(other_sum, CORES)
        for i, k in enumerate(distances):
            for h in range(2):
                part = slice(8 * h, 8 * h + 8)
                sums[k, h] = own_sum[i, part].astype(F32) + other_sum[i, part].astype(F32)

    def send(k):
        nonlocal flags
        ups = {(k, h): sums[k, h] + (up[k + 1, h].astype(F32) if (k + 1, h) in up else 0.0) for h in range(2) if k < 4 or h == 0}
        downs = {(k, h): sums[8 - k, h] + (down[k + 1, h].astype(F32) if (k + 1, h) in down else 0.0) for h in range(2) if k < 4 or h == 1}
        ups, downs = [{key: t.astype(BF) for key, t in part.items()} for part in (ups, downs)]
        flags, ups, downs = lax.optimization_barrier((flags, ups, downs))
        up.update({key: hop(t, UP) for key, t in ups.items()})
        down.update({key: hop(t, DOWN) for key, t in downs.items()})

    add_up([4])
    add_up([3, 5])
    send(4)
    add_up([2, 6, 1, 7, 0])
    send(3)
    send(2)
    send(1)
    owned = jnp.concatenate([sums[0, h] + up[1, h].astype(F32) + down[1, h].astype(F32) for h in range(2)], axis=0)
    new_momentum = momentum_decay * momentum + owned[None]
    new_master = master - step_size * new_momentum
    return new_master, new_momentum, new_res.reshape(residual.shape)


def local_plain(tokens, out_grad, master, momentum, residual, kept_blocks):
    whole_in = lax.all_gather(tokens, "mp", axis=1, tiled=True)
    whole_grad = lax.all_gather(out_grad, "mp", axis=1, tiled=True)
    tile = master.shape[-1]
    width = whole_in.shape[1]
    block_count = residual.shape[2]
    half = block_count // 2
    rows = width // tile
    cols = half // rows
    working = lax.all_gather(master.astype(BF), "dp", axis=1, tiled=True)[0]
    first_w = working[:half].reshape(rows, cols, tile, tile).transpose(0, 2, 1, 3).reshape(width, cols * tile)
    second_w = working[half:].reshape(cols, rows, tile, tile).transpose(0, 2, 1, 3).reshape(cols * tile, width)
    pre = jnp.dot(whole_in, first_w, preferred_element_type=F32)
    act_full, pullback = jax.vjp(activation, pre)
    act = act_full.astype(BF)
    act_grad = jnp.dot(whole_grad, second_w.T, preferred_element_type=F32)
    hid = pullback(act_grad)[0].astype(BF)
    first_g = jnp.dot(whole_in.T, hid, preferred_element_type=F32)
    second_g = jnp.dot(act.T, whole_grad, preferred_element_type=F32)
    first_g = first_g.reshape(rows, tile, cols, tile).transpose(0, 2, 1, 3).reshape(half, tile, tile)
    second_g = second_g.reshape(cols, tile, rows, tile).transpose(0, 2, 1, 3).reshape(half, tile, tile)
    grads = jnp.concatenate([first_g, second_g], axis=0) + residual[0, 0].astype(F32)
    flags = jnp.any(jnp.arange(block_count, dtype=jnp.int32)[None, :] == kept_blocks[0, 0][:, None], axis=0)
    flags = flags[:, None, None]
    new_residual = jnp.where(flags, 0.0, grads).astype(BF)[None, None]
    owned = lax.psum_scatter(jnp.where(flags, grads, 0.0), "dp", scatter_dimension=0, tiled=True)
    new_momentum = momentum_decay * momentum + owned[None]
    return master - step_size * new_momentum, new_momentum, new_residual


def solution(mesh):
    ring = mesh.shape["dp"] == 16 and mesh.shape["mp"] == 2
    blocks = P("mp", "dp", None, None)
    left = P("dp", "mp", None, None, None)
    return jax.shard_map(
        local_ring if ring else local_plain,
        mesh=mesh,
        in_specs=(P("dp", "mp"), P("dp", "mp"), blocks, blocks, left, P("dp", "mp", None)),
        out_specs=(blocks, blocks, left),
        check_vma=False,
    )
```

```python
import functools

import jax
import jax.numpy as jnp
from jax import lax
from jax.experimental import pallas as pl
from jax.experimental.pallas import tpu as pltpu
from jax.sharding import PartitionSpec as P

momentum_decay = 0.9
step_size = 0.01
BF = jnp.bfloat16
F32 = jnp.float32
ANY = pl.BlockSpec(memory_space=pl.ANY)
HBM = pltpu.HBM
VMEM = pltpu.VMEM
GELU_S = 0.7978845608028654
GELU_C = 0.044715


def activation(values):
    return jax.nn.gelu(values, approximate=True)


def in_hbm(array):
    return pltpu.with_memory_space_constraint(array, HBM)


def in_vmem(array):
    return pltpu.with_memory_space_constraint(array, VMEM)


def gelu_and_slope(v):
    sq = v * v
    t = jnp.tanh(v * (GELU_S + (GELU_S * GELU_C) * sq))
    half = 0.5 + 0.5 * t
    act = v * half
    slope = half + act * (1.0 - t) * (GELU_S + (3.0 * GELU_S * GELU_C) * sq)
    return act, slope


def load_weight(halves, first, owners, srcs, dst, sem):
    shift = owners[len(halves)]
    for s, half in enumerate(halves):
        owner = owners[s]

        @pl.when((owner < 8) if first else (owner >= 8))
        def _(s=s, half=half, owner=owner):
            if first:
                row = pl.multiple_of(((owner - shift) & 7) * 128, 128)
                slots = pl.ds(0, 16) if half is None else pl.ds(8 * half, 8)
                pltpu.make_async_copy(srcs[s], dst.at[slots, pl.ds(row, 128)], sem).start()
                return
            for i in (0, 1) if half is None else (half,):
                row = pl.multiple_of((owner - 8) * 256 + 128 * i, 128)
                src = srcs[s].at[pl.ds(8 * i, 8)] if half is None else srcs[s]
                pltpu.make_async_copy(src, dst.at[:, pl.ds(row, 128)], sem).start()


def pre_kernel(halves, owners, x_own, *refs):
    units, (x_other, left_t, slope_ref, w1, sem) = refs[: len(halves)], refs[len(halves) :]
    step = pl.program_id(0)
    rows = x_own.shape[0]

    @pl.when(step == 0)
    def _():
        load_weight(halves, True, owners, units, w1, sem)

    for s in range(4):

        @pl.when(step == s)
        def _(s=s):
            lanes = slice(256 * (s % 2), 256 * (s % 2) + 256)
            left_t[...] = (x_own if s < 2 else x_other)[:, lanes].T

    @pl.when(step == 4)
    def _():
        pltpu.make_async_copy(w1, w1, sem).wait()

    @pl.when(step >= 4)
    def _():
        c = 2 * (step - 4)
        w = jnp.concatenate([w1[c], w1[c + 1]], axis=1)
        block = rows // 4

        def product(r):
            pre = jnp.dot(x_own[r : r + block, :], w[: w.shape[0] // 2], preferred_element_type=F32)
            return pre + jnp.dot(x_other[r : r + block, :], w[w.shape[0] // 2 :], preferred_element_type=F32)

        starts = list(range(0, rows, block))
        ahead = product(starts[0])
        for i, r in enumerate(starts):
            pre = ahead
            if i + 1 < len(starts):
                ahead = product(starts[i + 1])
            act, slope = gelu_and_slope(pre)
            left_t[:, r : r + block] = act.astype(BF).T
            slope_ref[0, r : r + block, :] = slope


def hid_first_kernel(halves, owners, dy_own, dy_other, slope_ref, *refs):
    units, (right, w2_t, w2, sem) = refs[: len(halves)], refs[len(halves) :]
    step = pl.program_id(0)
    shift = owners[len(halves)]

    @pl.when(step == 0)
    def _():
        load_weight(halves, False, owners, units, w2, sem)

    @pl.when(step == 2)
    def _():
        pltpu.make_async_copy(w2, w2, sem).wait()

    @pl.when(step >= 2)
    def _():
        for j in range(2):
            row = pl.multiple_of(512 * (step - 2) + 256 * j, 256)
            for c in range(8):
                w2_t[j, 128 * c : 128 * c + 128, :] = w2[(c + shift) & 7, pl.ds(row, 256), :].T

    hid_block(dy_own, dy_other, w2_t, slope_ref, right)


def hid_block(dy_own, dy_other, w2_t, slope_ref, right):
    step = pl.program_id(0)
    skip = dy_other.shape[0] - dy_own.shape[0]

    @pl.when(step < 2)
    def _():
        for j in range(2):
            lanes = slice(256 * j, 256 * j + 256)
            right[j] = jnp.where(step == 0, dy_own[:, lanes], dy_other[skip:, lanes])

    @pl.when(step >= 2)
    def _():
        half = w2_t.shape[1] // 2
        for j in range(2):
            g = jnp.dot(dy_own[...], w2_t[j, :half, :], preferred_element_type=F32)
            g += jnp.dot(dy_other[skip:, :], w2_t[j, half:, :], preferred_element_type=F32)
            right[j] = (g * slope_ref[j]).astype(BF)


def hid_second_kernel(dy_own, dy_other, slope_ref, w2_t, _, right):
    hid_block(dy_own, dy_other, w2_t, slope_ref, right)


def grad_kernel(layout, info, flags, left_ref, right_ref, res_ref, *refs):
    new_res, *sent, held, sems = refs[len(refs) - 2 * len(layout) - 3 :]
    places = [(array, i) for array, size in enumerate(layout) for i in range(size)]
    count = len(places)
    group, h = pl.program_id(0), pl.program_id(1)
    slot_now = group & 1
    mine, other = held.at[slot_now, 0], held.at[slot_now, 1]

    def copy_out(slot, which, k):
        array, i = places[k]
        return pltpu.make_async_copy(held.at[slot, which], sent[2 * array + which].at[i], sems.at[slot, which])

    @pl.when((h == 0) & (group >= 2))
    def _():
        for which in range(2):
            copy_out(slot_now, which, 0).wait()

    g = info[2 * group]
    row = pl.multiple_of(256 * (info[2 * group + 1] + jnp.where(g < 4, 0, h + 4)), 256)
    left = left_ref.at[pl.ds(row, 256)]
    shift, core = info[info.shape[0] - 2], info[info.shape[0] - 1]
    dot = functools.partial(jnp.dot, preferred_element_type=F32)

    def finish(value, flat):
        kept = flags[32 * g + flat] != 0
        value = value + res_ref[0, flat].astype(F32)
        new_res[0, flat] = jnp.where(kept, 0.0, value).astype(BF)
        return jnp.where(kept, value, 0.0).astype(BF)

    @pl.when(g < 4)
    def _():
        for c in range(4):
            grad = dot(left[...], right_ref[4 * h + c])
            for out, row in ((mine, core), (other, 1 - core)):
                for j in range(2):
                    lanes = slice(128 * j, 128 * j + 128)
                    slot = 8 * h + 2 * c + j
                    out[slot] = finish(jnp.where(row == 0, grad[:128, lanes], grad[128:, lanes]), 16 * row + slot)

    for out, here in ((mine, h == core), (other, h != core)):

        @pl.when((g >= 4) & here)
        def _(out=out):
            for c in range(4):
                grad = dot(left[...], right_ref[8 + c])
                for i in range(2):
                    for j in range(2):
                        slot = 8 * i + ((2 * c + j + shift) & 7)
                        out[slot] = finish(grad[128 * i : 128 * i + 128, 128 * j : 128 * j + 128], 16 * h + slot)

    for k in range(count):

        @pl.when((h == 1) & (group == k))
        def _(k=k):
            for which in range(2):
                copy_out(k & 1, which, k).start()

    @pl.when((h == 1) & (group == count - 1))
    def _():
        for k in range(max(count - 2, 0), count):
            for which in range(2):
                copy_out(k & 1, which, k).wait()


def run_pre(owners, halves, x_own, x_other, units):
    rows = x_own.shape[0]
    whole = lambda t: pl.BlockSpec(t.shape, lambda i, *_: (0, 0))
    return pl.pallas_call(
        functools.partial(pre_kernel, halves),
        grid_spec=pltpu.PrefetchScalarGridSpec(
            num_scalar_prefetch=1,
            grid=(12,),
            in_specs=[whole(x_own)] + [ANY] * len(units) + [whole(x_other)],
            out_specs=[
                pl.BlockSpec((256, rows), lambda i, *_: (i, 0)),
                pl.BlockSpec((1, rows, 256), lambda i, *_: (jnp.maximum(i - 4, 0), 0, 0)),
            ],
            scratch_shapes=[pltpu.VMEM((16, 1024, 128), BF), pltpu.SemaphoreType.DMA],
        ),
        out_shape=[VMEM((3072, rows), BF), HBM((8, rows, 256), F32)],
        compiler_params=pltpu.CompilerParams(vmem_limit_bytes=24 * 2**20),
        cost_estimate=pl.CostEstimate(flops=rows * 512 * 1024, bytes_accessed=2_000_000, transcendentals=0),
        name="pre_act",
    )(owners, in_hbm(x_own), *[in_hbm(u) for u in units], x_other)


def run_hid_first(owners, halves, dy_own, dy_other, slope, units):
    total = slope.shape[1]
    rows = total // 2
    later = lambda i: jnp.maximum(i - 2, 0)
    return pl.pallas_call(
        functools.partial(hid_first_kernel, halves),
        grid_spec=pltpu.PrefetchScalarGridSpec(
            num_scalar_prefetch=1,
            grid=(6,),
            in_specs=[
                pl.BlockSpec((rows, 512), lambda i, *_: (0, 0)),
                pl.BlockSpec(dy_other.shape, lambda i, *_: (0, 0)),
                pl.BlockSpec((2, rows, 256), lambda i, *_: (later(i), 0, 0)),
                *[ANY] * len(units),
            ],
            out_specs=[
                pl.BlockSpec((2, rows, 256), lambda i, *_: (jnp.where(i < 2, i + 4, i - 2), 0, 0)),
                pl.BlockSpec((2, 1024, 256), lambda i, *_: (later(i), 0, 0)),
            ],
            scratch_shapes=[pltpu.VMEM((8, 2048, 128), BF), pltpu.SemaphoreType.DMA],
        ),
        out_shape=[VMEM((12, total, 256), BF), VMEM((8, 1024, 256), BF)],
        compiler_params=pltpu.CompilerParams(vmem_limit_bytes=22 * 2**20),
        cost_estimate=pl.CostEstimate(flops=rows * 512 * 1024, bytes_accessed=2_000_000, transcendentals=0),
        name="hid_first",
    )(owners, in_hbm(dy_own), dy_other, in_hbm(slope), *[in_hbm(u) for u in units])


def run_hid_second(dy_own, dy_other, slope, w2_t, right):
    rows = dy_other.shape[0]
    later = lambda i: jnp.maximum(i - 2, 0)
    return pl.pallas_call(
        hid_second_kernel,
        grid=(6,),
        in_specs=[
            pl.BlockSpec((rows, 512), lambda i: (1, 0)),
            pl.BlockSpec((rows, 512), lambda i: (0, 0)),
            pl.BlockSpec((2, rows, 256), lambda i: (later(i), 1, 0)),
            pl.BlockSpec((2, 1024, 256), lambda i: (later(i), 0, 0)),
            ANY,
        ],
        out_specs=pl.BlockSpec((2, rows, 256), lambda i: (jnp.where(i < 2, i + 4, i - 2), 1, 0)),
        out_shape=VMEM(right.shape, BF),
        input_output_aliases={4: 0},
        compiler_params=pltpu.CompilerParams(vmem_limit_bytes=18 * 2**20),
        cost_estimate=pl.CostEstimate(flops=3 * rows * 1024 * 2048, bytes_accessed=15_000_000, transcendentals=0),
        name="hid_second",
    )(in_hbm(dy_own), dy_other, in_hbm(slope), in_vmem(w2_t), in_vmem(right))


def run_grads(info, flags, left_t, right, residual, new_res, layout):
    rows = right.shape[1]
    block = pl.BlockSpec((1, 32, 128, 128), lambda i, h, info, *_: (info[2 * i], 0, 0, 0))
    operands = [info, flags, in_vmem(left_t), in_vmem(right), in_hbm(residual)]
    specs = [
        pl.BlockSpec(left_t.shape, lambda i, h, *_: (0, 0)),
        pl.BlockSpec(right.shape, lambda i, h, *_: (0, 0, 0)),
        block,
    ]
    alias = {}
    if new_res is not None:
        alias = {len(operands): 0}
        operands.append(in_hbm(new_res))
        specs.append(ANY)
    count = sum(layout)
    sent = [HBM((size, 16, 128, 128), BF) for size in layout for _ in range(2)]
    return pl.pallas_call(
        functools.partial(grad_kernel, layout),
        grid_spec=pltpu.PrefetchScalarGridSpec(
            num_scalar_prefetch=2,
            grid=(count, 2),
            in_specs=specs,
            out_specs=[block] + [ANY] * len(sent),
            scratch_shapes=[pltpu.VMEM((2, 2, 16, 128, 128), BF), pltpu.SemaphoreType.DMA((2, 2))],
        ),
        out_shape=[HBM(residual.shape, BF), *sent],
        input_output_aliases=alias,
        compiler_params=pltpu.CompilerParams(vmem_limit_bytes=20 * 2**20),
        cost_estimate=pl.CostEstimate(flops=4 * rows * 1024 * 512 * count, bytes_accessed=10_000_000 * count, transcendentals=0),
        name="grad_blocks",
    )(*operands)


def chip_at(place):
    place = place % 8
    if isinstance(place, int):
        return 2 * place if place < 4 else 2 * (7 - place) + 1
    return jnp.where(place < 4, 2 * place, 2 * (7 - place) + 1)


def ring_pairs(step):
    return [(2 * chip_at(p) + c, 2 * chip_at(p + step) + c) for p in range(8) for c in range(2)]


UP, DOWN = ring_pairs(1), ring_pairs(-1)
CORES = [(i, i ^ 1) for i in range(16)]
PAIR = [(0, 1), (1, 0)]


def hop(array, pairs):
    return lax.ppermute(array, "dp", pairs)


def local_ring(tokens, out_grad, master, momentum, residual, kept_blocks):
    mine = lax.axis_index("dp").astype(jnp.int32)
    shard = lax.axis_index("mp").astype(jnp.int32)
    core = mine & 1
    chip = mine >> 1
    place = jnp.where((chip & 1) == 0, chip >> 1, 7 - (chip >> 1))
    rows = tokens.shape[0]

    half = rows // 2
    swap = lambda t: lax.ppermute(t, "mp", PAIR)
    x_other = swap(tokens)
    dy_early = swap(out_grad[:half])
    dy_late = swap(out_grad[half:])

    shift = 4 * shard
    own = master[0].astype(BF)
    up = down = own
    units, halves, owners = [own], [None], [mine]
    for k in range(1, 5):
        if k == 4:
            x_other, up, down = lax.optimization_barrier((x_other, up, down))
        if k == 4:
            up, down = up[:8], down[8:]
        up, down = hop(up, UP), hop(down, DOWN)
        halves += [0, 1] if k == 4 else [None, None]
        units += [up, down]
        owners += [2 * chip_at(place - k) + core, 2 * chip_at(place + k) + core]
    units = units + [hop(u, CORES) for u in units]
    halves = tuple(halves * 2)
    owners = jnp.stack(owners + [o ^ 1 for o in owners] + [shift])

    block_count = residual.shape[2]
    flags = jnp.any(jnp.arange(block_count, dtype=jnp.int32)[None, :] == kept_blocks[0, 0][:, None], axis=0)
    flags = flags.astype(jnp.int32)

    left_t, slope = run_pre(owners, halves, tokens, x_other, units)
    right, w2_t = run_hid_first(owners, halves, out_grad, dy_early, slope, units)
    right = run_hid_second(out_grad, dy_late, slope, w2_t, right)

    stored = residual.reshape(8, 32, 128, 128)

    def info_of(distances):
        out = []
        for k in distances:
            g = chip_at(place + k)
            a = jnp.where(g < 4, (g - 2 * shard) & 3, 2 * (g - 4))
            out += [g, a]
        return jnp.stack(out + [shift, core])

    new_res, sums, up, down = None, {}, {}, {}

    def add_up(*arrays):
        nonlocal new_res
        new_res, *sent = run_grads(
            info_of(sum(arrays, [])), flags, left_t, right, stored, new_res, tuple(len(t) for t in arrays)
        )
        for a, distances in enumerate(arrays):
            own_sum, other_sum = sent[2 * a], hop(sent[2 * a + 1], CORES)
            for i, k in enumerate(distances):
                for h in range(2):
                    part = slice(8 * h, 8 * h + 8)
                    sums[k, h] = own_sum[i, part].astype(F32) + other_sum[i, part].astype(F32)

    def send(k):
        nonlocal flags
        ups = {(k, h): sums[k, h] + (up[k + 1, h].astype(F32) if (k + 1, h) in up else 0.0) for h in range(2) if k < 4 or h == 0}
        downs = {(k, h): sums[8 - k, h] + (down[k + 1, h].astype(F32) if (k + 1, h) in down else 0.0) for h in range(2) if k < 4 or h == 1}
        ups, downs = [{key: t.astype(BF) for key, t in part.items()} for part in (ups, downs)]
        flags, ups, downs = lax.optimization_barrier((flags, ups, downs))
        up.update({key: hop(t, UP) for key, t in ups.items()})
        down.update({key: hop(t, DOWN) for key, t in downs.items()})

    add_up([4])
    add_up([3, 5])
    send(4)
    add_up([2, 6], [1, 7, 0])
    send(3)
    send(2)
    send(1)
    owned = jnp.concatenate([sums[0, h] + up[1, h].astype(F32) + down[1, h].astype(F32) for h in range(2)], axis=0)
    new_momentum = momentum_decay * momentum + owned[None]
    new_master = master - step_size * new_momentum
    return new_master, new_momentum, new_res.reshape(residual.shape)


def local_plain(tokens, out_grad, master, momentum, residual, kept_blocks):
    whole_in = lax.all_gather(tokens, "mp", axis=1, tiled=True)
    whole_grad = lax.all_gather(out_grad, "mp", axis=1, tiled=True)
    tile = master.shape[-1]
    width = whole_in.shape[1]
    block_count = residual.shape[2]
    half = block_count // 2
    rows = width // tile
    cols = half // rows
    working = lax.all_gather(master.astype(BF), "dp", axis=1, tiled=True)[0]
    first_w = working[:half].reshape(rows, cols, tile, tile).transpose(0, 2, 1, 3).reshape(width, cols * tile)
    second_w = working[half:].reshape(cols, rows, tile, tile).transpose(0, 2, 1, 3).reshape(cols * tile, width)
    pre = jnp.dot(whole_in, first_w, preferred_element_type=F32)
    act_full, pullback = jax.vjp(activation, pre)
    act = act_full.astype(BF)
    act_grad = jnp.dot(whole_grad, second_w.T, preferred_element_type=F32)
    hid = pullback(act_grad)[0].astype(BF)
    first_g = jnp.dot(whole_in.T, hid, preferred_element_type=F32)
    second_g = jnp.dot(act.T, whole_grad, preferred_element_type=F32)
    first_g = first_g.reshape(rows, tile, cols, tile).transpose(0, 2, 1, 3).reshape(half, tile, tile)
    second_g = second_g.reshape(cols, tile, rows, tile).transpose(0, 2, 1, 3).reshape(half, tile, tile)
    grads = jnp.concatenate([first_g, second_g], axis=0) + residual[0, 0].astype(F32)
    flags = jnp.any(jnp.arange(block_count, dtype=jnp.int32)[None, :] == kept_blocks[0, 0][:, None], axis=0)
    flags = flags[:, None, None]
    new_residual = jnp.where(flags, 0.0, grads).astype(BF)[None, None]
    owned = lax.psum_scatter(jnp.where(flags, grads, 0.0), "dp", scatter_dimension=0, tiled=True)
    new_momentum = momentum_decay * momentum + owned[None]
    return master - step_size * new_momentum, new_momentum, new_residual


def solution(mesh):
    ring = mesh.shape["dp"] == 16 and mesh.shape["mp"] == 2
    blocks = P("mp", "dp", None, None)
    left = P("dp", "mp", None, None, None)
    return jax.shard_map(
        local_ring if ring else local_plain,
        mesh=mesh,
        in_specs=(P("dp", "mp"), P("dp", "mp"), blocks, blocks, left, P("dp", "mp", None)),
        out_specs=(blocks, blocks, left),
        check_vma=False,
    )
```

```python
import functools

import jax
import jax.numpy as jnp
from jax import lax
from jax.experimental import pallas as pl
from jax.experimental.pallas import tpu as pltpu
from jax.sharding import PartitionSpec as P

momentum_decay = 0.9
step_size = 0.01
BF = jnp.bfloat16
F32 = jnp.float32
ANY = pl.BlockSpec(memory_space=pl.ANY)
HBM = pltpu.HBM
VMEM = pltpu.VMEM
GELU_S = 0.7978845608028654
GELU_C = 0.044715


def activation(values):
    return jax.nn.gelu(values, approximate=True)


def in_hbm(array):
    return pltpu.with_memory_space_constraint(array, HBM)


def in_vmem(array):
    return pltpu.with_memory_space_constraint(array, VMEM)


def gelu_and_slope(v):
    sq = v * v
    t = jnp.tanh(v * (GELU_S + (GELU_S * GELU_C) * sq))
    half = 0.5 + 0.5 * t
    act = v * half
    slope = half + act * (1.0 - t) * (GELU_S + (3.0 * GELU_S * GELU_C) * sq)
    return act, slope


def load_weight(halves, first, owners, srcs, dst, sem):
    shift = owners[len(halves)]
    for s, half in enumerate(halves):
        owner = owners[s]

        @pl.when((owner < 8) if first else (owner >= 8))
        def _(s=s, half=half, owner=owner):
            if first:
                row = pl.multiple_of(((owner - shift) & 7) * 128, 128)
                slots = pl.ds(0, 16) if half is None else pl.ds(8 * half, 8)
                pltpu.make_async_copy(srcs[s], dst.at[slots, pl.ds(row, 128)], sem).start()
                return
            for i in (0, 1) if half is None else (half,):
                row = pl.multiple_of((owner - 8) * 256 + 128 * i, 128)
                src = srcs[s].at[pl.ds(8 * i, 8)] if half is None else srcs[s]
                pltpu.make_async_copy(src, dst.at[:, pl.ds(row, 128)], sem).start()


def pre_kernel(halves, owners, x_own, *refs):
    units, (x_other, left_t, slope_ref, w1, sem) = refs[: len(halves)], refs[len(halves) :]
    step = pl.program_id(0)
    rows = x_own.shape[0]

    @pl.when(step == 0)
    def _():
        load_weight(halves, True, owners, units, w1, sem)

    for s in range(4):

        @pl.when(step == s)
        def _(s=s):
            lanes = slice(256 * (s % 2), 256 * (s % 2) + 256)
            left_t[...] = (x_own if s < 2 else x_other)[:, lanes].T

    @pl.when(step == 4)
    def _():
        pltpu.make_async_copy(w1, w1, sem).wait()

    @pl.when(step >= 4)
    def _():
        c = 2 * (step - 4)
        w = jnp.concatenate([w1[c], w1[c + 1]], axis=1)
        block = rows // 3

        def product(r):
            pre = jnp.dot(x_own[r : r + block, :], w[: w.shape[0] // 2], preferred_element_type=F32)
            return pre + jnp.dot(x_other[r : r + block, :], w[w.shape[0] // 2 :], preferred_element_type=F32)

        starts = list(range(0, rows, block))
        ahead = product(starts[0])
        for i, r in enumerate(starts):
            pre = ahead
            if i + 1 < len(starts):
                ahead = product(starts[i + 1])
            act, slope = gelu_and_slope(pre)
            left_t[:, r : r + block] = act.astype(BF).T
            slope_ref[0, r : r + block, :] = slope


def hid_first_kernel(halves, owners, dy_own, dy_other, slope_ref, *refs):
    units, (right, w2_t, w2, sem) = refs[: len(halves)], refs[len(halves) :]
    step = pl.program_id(0)
    shift = owners[len(halves)]

    @pl.when(step == 0)
    def _():
        load_weight(halves, False, owners, units, w2, sem)

    @pl.when(step == 2)
    def _():
        pltpu.make_async_copy(w2, w2, sem).wait()

    @pl.when(step >= 2)
    def _():
        for j in range(2):
            row = pl.multiple_of(512 * (step - 2) + 256 * j, 256)
            for c in range(8):
                w2_t[j, 128 * c : 128 * c + 128, :] = w2[(c + shift) & 7, pl.ds(row, 256), :].T

    hid_block(dy_own, dy_other, w2_t, slope_ref, right)


def hid_block(dy_own, dy_other, w2_t, slope_ref, right):
    step = pl.program_id(0)
    skip = dy_other.shape[0] - dy_own.shape[0]

    @pl.when(step < 2)
    def _():
        for j in range(2):
            lanes = slice(256 * j, 256 * j + 256)
            right[j] = jnp.where(step == 0, dy_own[:, lanes], dy_other[skip:, lanes])

    @pl.when(step >= 2)
    def _():
        half = w2_t.shape[1] // 2
        for j in range(2):
            g = jnp.dot(dy_own[...], w2_t[j, :half, :], preferred_element_type=F32)
            g += jnp.dot(dy_other[skip:, :], w2_t[j, half:, :], preferred_element_type=F32)
            right[j] = (g * slope_ref[j]).astype(BF)


def hid_second_kernel(dy_own, dy_other, slope_ref, w2_t, _, right):
    hid_block(dy_own, dy_other, w2_t, slope_ref, right)


def grad_kernel(layout, info, flags, left_ref, right_ref, res_ref, *refs):
    new_res, *sent, held, sems = refs[len(refs) - 2 * len(layout) - 3 :]
    places = [(array, i) for array, size in enumerate(layout) for i in range(size)]
    count = len(places)
    group, h = pl.program_id(0), pl.program_id(1)
    slot_now = group & 1
    mine, other = held.at[slot_now, 0], held.at[slot_now, 1]

    def copy_out(slot, which, k):
        array, i = places[k]
        return pltpu.make_async_copy(held.at[slot, which], sent[2 * array + which].at[i], sems.at[slot, which])

    @pl.when((h == 0) & (group >= 2))
    def _():
        for which in range(2):
            copy_out(slot_now, which, 0).wait()

    g = info[2 * group]
    row = pl.multiple_of(256 * (info[2 * group + 1] + jnp.where(g < 4, 0, h + 4)), 256)
    left = left_ref.at[pl.ds(row, 256)]
    shift, core = info[info.shape[0] - 2], info[info.shape[0] - 1]
    dot = functools.partial(jnp.dot, preferred_element_type=F32)

    def finish(value, flat):
        kept = flags[32 * g + flat] != 0
        value = value + res_ref[0, flat].astype(F32)
        new_res[0, flat] = jnp.where(kept, 0.0, value).astype(BF)
        return jnp.where(kept, value, 0.0).astype(BF)

    @pl.when(g < 4)
    def _():
        for c in range(4):
            grad = dot(left[...], right_ref[4 * h + c])
            for out, row in ((mine, core), (other, 1 - core)):
                for j in range(2):
                    lanes = slice(128 * j, 128 * j + 128)
                    slot = 8 * h + 2 * c + j
                    out[slot] = finish(jnp.where(row == 0, grad[:128, lanes], grad[128:, lanes]), 16 * row + slot)

    for out, here in ((mine, h == core), (other, h != core)):

        @pl.when((g >= 4) & here)
        def _(out=out):
            for c in range(4):
                grad = dot(left[...], right_ref[8 + c])
                for i in range(2):
                    for j in range(2):
                        slot = 8 * i + ((2 * c + j + shift) & 7)
                        out[slot] = finish(grad[128 * i : 128 * i + 128, 128 * j : 128 * j + 128], 16 * h + slot)

    for k in range(count):

        @pl.when((h == 1) & (group == k))
        def _(k=k):
            for which in range(2):
                copy_out(k & 1, which, k).start()

    @pl.when((h == 1) & (group == count - 1))
    def _():
        for k in range(max(count - 2, 0), count):
            for which in range(2):
                copy_out(k & 1, which, k).wait()


def run_pre(owners, halves, x_own, x_other, units):
    rows = x_own.shape[0]
    whole = lambda t: pl.BlockSpec(t.shape, lambda i, *_: (0, 0))
    return pl.pallas_call(
        functools.partial(pre_kernel, halves),
        grid_spec=pltpu.PrefetchScalarGridSpec(
            num_scalar_prefetch=1,
            grid=(12,),
            in_specs=[whole(x_own)] + [ANY] * len(units) + [whole(x_other)],
            out_specs=[
                pl.BlockSpec((256, rows), lambda i, *_: (i, 0)),
                pl.BlockSpec((1, rows, 256), lambda i, *_: (jnp.maximum(i - 4, 0), 0, 0)),
            ],
            scratch_shapes=[pltpu.VMEM((16, 1024, 128), BF), pltpu.SemaphoreType.DMA],
        ),
        out_shape=[VMEM((3072, rows), BF), HBM((8, rows, 256), F32)],
        compiler_params=pltpu.CompilerParams(vmem_limit_bytes=24 * 2**20),
        cost_estimate=pl.CostEstimate(flops=rows * 512 * 1024, bytes_accessed=2_000_000, transcendentals=0),
        name="pre_act",
    )(owners, in_hbm(x_own), *[in_hbm(u) for u in units], x_other)


def run_hid_first(owners, halves, dy_own, dy_other, slope, units):
    total = slope.shape[1]
    rows = total // 2
    later = lambda i: jnp.maximum(i - 2, 0)
    return pl.pallas_call(
        functools.partial(hid_first_kernel, halves),
        grid_spec=pltpu.PrefetchScalarGridSpec(
            num_scalar_prefetch=1,
            grid=(6,),
            in_specs=[
                pl.BlockSpec((rows, 512), lambda i, *_: (0, 0)),
                pl.BlockSpec(dy_other.shape, lambda i, *_: (0, 0)),
                pl.BlockSpec((2, rows, 256), lambda i, *_: (later(i), 0, 0)),
                *[ANY] * len(units),
            ],
            out_specs=[
                pl.BlockSpec((2, rows, 256), lambda i, *_: (jnp.where(i < 2, i + 4, i - 2), 0, 0)),
                pl.BlockSpec((2, 1024, 256), lambda i, *_: (later(i), 0, 0)),
            ],
            scratch_shapes=[pltpu.VMEM((8, 2048, 128), BF), pltpu.SemaphoreType.DMA],
        ),
        out_shape=[VMEM((12, total, 256), BF), VMEM((8, 1024, 256), BF)],
        compiler_params=pltpu.CompilerParams(vmem_limit_bytes=22 * 2**20),
        cost_estimate=pl.CostEstimate(flops=rows * 512 * 1024, bytes_accessed=2_000_000, transcendentals=0),
        name="hid_first",
    )(owners, in_hbm(dy_own), dy_other, in_hbm(slope), *[in_hbm(u) for u in units])


def run_hid_second(dy_own, dy_other, slope, w2_t, right):
    rows = dy_other.shape[0]
    later = lambda i: jnp.maximum(i - 2, 0)
    return pl.pallas_call(
        hid_second_kernel,
        grid=(6,),
        in_specs=[
            pl.BlockSpec((rows, 512), lambda i: (1, 0)),
            pl.BlockSpec((rows, 512), lambda i: (0, 0)),
            pl.BlockSpec((2, rows, 256), lambda i: (later(i), 1, 0)),
            pl.BlockSpec((2, 1024, 256), lambda i: (later(i), 0, 0)),
            ANY,
        ],
        out_specs=pl.BlockSpec((2, rows, 256), lambda i: (jnp.where(i < 2, i + 4, i - 2), 1, 0)),
        out_shape=VMEM(right.shape, BF),
        input_output_aliases={4: 0},
        compiler_params=pltpu.CompilerParams(vmem_limit_bytes=18 * 2**20),
        cost_estimate=pl.CostEstimate(flops=3 * rows * 1024 * 2048, bytes_accessed=15_000_000, transcendentals=0),
        name="hid_second",
    )(in_hbm(dy_own), dy_other, in_hbm(slope), in_vmem(w2_t), in_vmem(right))


def run_grads(info, flags, left_t, right, residual, new_res, layout):
    rows = right.shape[1]
    block = pl.BlockSpec((1, 32, 128, 128), lambda i, h, info, *_: (info[2 * i], 0, 0, 0))
    operands = [info, flags, in_vmem(left_t), in_vmem(right), in_hbm(residual)]
    specs = [
        pl.BlockSpec(left_t.shape, lambda i, h, *_: (0, 0)),
        pl.BlockSpec(right.shape, lambda i, h, *_: (0, 0, 0)),
        block,
    ]
    alias = {}
    if new_res is not None:
        alias = {len(operands): 0}
        operands.append(in_hbm(new_res))
        specs.append(ANY)
    count = sum(layout)
    sent = [HBM((size, 16, 128, 128), BF) for size in layout for _ in range(2)]
    return pl.pallas_call(
        functools.partial(grad_kernel, layout),
        grid_spec=pltpu.PrefetchScalarGridSpec(
            num_scalar_prefetch=2,
            grid=(count, 2),
            in_specs=specs,
            out_specs=[block] + [ANY] * len(sent),
            scratch_shapes=[pltpu.VMEM((2, 2, 16, 128, 128), BF), pltpu.SemaphoreType.DMA((2, 2))],
        ),
        out_shape=[HBM(residual.shape, BF), *sent],
        input_output_aliases=alias,
        compiler_params=pltpu.CompilerParams(vmem_limit_bytes=20 * 2**20),
        cost_estimate=pl.CostEstimate(flops=4 * rows * 1024 * 512 * count, bytes_accessed=10_000_000 * count, transcendentals=0),
        name="grad_blocks",
    )(*operands)


def chip_at(place):
    place = place % 8
    if isinstance(place, int):
        return 2 * place if place < 4 else 2 * (7 - place) + 1
    return jnp.where(place < 4, 2 * place, 2 * (7 - place) + 1)


def ring_pairs(step):
    return [(2 * chip_at(p) + c, 2 * chip_at(p + step) + c) for p in range(8) for c in range(2)]


UP, DOWN = ring_pairs(1), ring_pairs(-1)
CORES = [(i, i ^ 1) for i in range(16)]
PAIR = [(0, 1), (1, 0)]


def hop(array, pairs):
    return lax.ppermute(array, "dp", pairs)


def local_ring(tokens, out_grad, master, momentum, residual, kept_blocks):
    mine = lax.axis_index("dp").astype(jnp.int32)
    shard = lax.axis_index("mp").astype(jnp.int32)
    core = mine & 1
    chip = mine >> 1
    place = jnp.where((chip & 1) == 0, chip >> 1, 7 - (chip >> 1))
    rows = tokens.shape[0]

    half = rows // 2
    swap = lambda t: lax.ppermute(t, "mp", PAIR)
    x_other = swap(tokens)
    dy_early = swap(out_grad[:half])
    dy_late = swap(out_grad[half:])

    shift = 4 * shard
    own = master[0].astype(BF)
    up = down = own
    units, halves, owners = [own], [None], [mine]
    for k in range(1, 5):
        if k == 4:
            x_other, up, down = lax.optimization_barrier((x_other, up, down))
        if k == 4:
            up, down = up[:8], down[8:]
        up, down = hop(up, UP), hop(down, DOWN)
        halves += [0, 1] if k == 4 else [None, None]
        units += [up, down]
        owners += [2 * chip_at(place - k) + core, 2 * chip_at(place + k) + core]
    units = units + [hop(u, CORES) for u in units]
    halves = tuple(halves * 2)
    owners = jnp.stack(owners + [o ^ 1 for o in owners] + [shift])

    block_count = residual.shape[2]
    flags = jnp.any(jnp.arange(block_count, dtype=jnp.int32)[None, :] == kept_blocks[0, 0][:, None], axis=0)
    flags = flags.astype(jnp.int32)

    left_t, slope = run_pre(owners, halves, tokens, x_other, units)
    right, w2_t = run_hid_first(owners, halves, out_grad, dy_early, slope, units)
    right = run_hid_second(out_grad, dy_late, slope, w2_t, right)

    stored = residual.reshape(8, 32, 128, 128)

    def info_of(distances):
        out = []
        for k in distances:
            g = chip_at(place + k)
            a = jnp.where(g < 4, (g - 2 * shard) & 3, 2 * (g - 4))
            out += [g, a]
        return jnp.stack(out + [shift, core])

    new_res, sums, up, down = None, {}, {}, {}

    def add_up(*arrays):
        nonlocal new_res
        new_res, *sent = run_grads(
            info_of(sum(arrays, [])), flags, left_t, right, stored, new_res, tuple(len(t) for t in arrays)
        )
        for a, distances in enumerate(arrays):
            own_sum, other_sum = sent[2 * a], hop(sent[2 * a + 1], CORES)
            for i, k in enumerate(distances):
                for h in range(2):
                    part = slice(8 * h, 8 * h + 8)
                    sums[k, h] = own_sum[i, part].astype(F32) + other_sum[i, part].astype(F32)

    def send(k):
        nonlocal flags
        ups = {(k, h): sums[k, h] + (up[k + 1, h].astype(F32) if (k + 1, h) in up else 0.0) for h in range(2) if k < 4 or h == 0}
        downs = {(k, h): sums[8 - k, h] + (down[k + 1, h].astype(F32) if (k + 1, h) in down else 0.0) for h in range(2) if k < 4 or h == 1}
        ups, downs = [{key: t.astype(BF) for key, t in part.items()} for part in (ups, downs)]
        flags, ups, downs = lax.optimization_barrier((flags, ups, downs))
        up.update({key: hop(t, UP) for key, t in ups.items()})
        down.update({key: hop(t, DOWN) for key, t in downs.items()})

    add_up([4])
    add_up([3, 5])
    send(4)
    add_up([2, 6], [1, 7, 0])
    send(3)
    send(2)
    send(1)
    owned = jnp.concatenate([sums[0, h] + up[1, h].astype(F32) + down[1, h].astype(F32) for h in range(2)], axis=0)
    new_momentum = momentum_decay * momentum + owned[None]
    new_master = master - step_size * new_momentum
    return new_master, new_momentum, new_res.reshape(residual.shape)


def local_plain(tokens, out_grad, master, momentum, residual, kept_blocks):
    whole_in = lax.all_gather(tokens, "mp", axis=1, tiled=True)
    whole_grad = lax.all_gather(out_grad, "mp", axis=1, tiled=True)
    tile = master.shape[-1]
    width = whole_in.shape[1]
    block_count = residual.shape[2]
    half = block_count // 2
    rows = width // tile
    cols = half // rows
    working = lax.all_gather(master.astype(BF), "dp", axis=1, tiled=True)[0]
    first_w = working[:half].reshape(rows, cols, tile, tile).transpose(0, 2, 1, 3).reshape(width, cols * tile)
    second_w = working[half:].reshape(cols, rows, tile, tile).transpose(0, 2, 1, 3).reshape(cols * tile, width)
    pre = jnp.dot(whole_in, first_w, preferred_element_type=F32)
    act_full, pullback = jax.vjp(activation, pre)
    act = act_full.astype(BF)
    act_grad = jnp.dot(whole_grad, second_w.T, preferred_element_type=F32)
    hid = pullback(act_grad)[0].astype(BF)
    first_g = jnp.dot(whole_in.T, hid, preferred_element_type=F32)
    second_g = jnp.dot(act.T, whole_grad, preferred_element_type=F32)
    first_g = first_g.reshape(rows, tile, cols, tile).transpose(0, 2, 1, 3).reshape(half, tile, tile)
    second_g = second_g.reshape(cols, tile, rows, tile).transpose(0, 2, 1, 3).reshape(half, tile, tile)
    grads = jnp.concatenate([first_g, second_g], axis=0) + residual[0, 0].astype(F32)
    flags = jnp.any(jnp.arange(block_count, dtype=jnp.int32)[None, :] == kept_blocks[0, 0][:, None], axis=0)
    flags = flags[:, None, None]
    new_residual = jnp.where(flags, 0.0, grads).astype(BF)[None, None]
    owned = lax.psum_scatter(jnp.where(flags, grads, 0.0), "dp", scatter_dimension=0, tiled=True)
    new_momentum = momentum_decay * momentum + owned[None]
    return master - step_size * new_momentum, new_momentum, new_residual


def solution(mesh):
    ring = mesh.shape["dp"] == 16 and mesh.shape["mp"] == 2
    blocks = P("mp", "dp", None, None)
    left = P("dp", "mp", None, None, None)
    return jax.shard_map(
        local_ring if ring else local_plain,
        mesh=mesh,
        in_specs=(P("dp", "mp"), P("dp", "mp"), blocks, blocks, left, P("dp", "mp", None)),
        out_specs=(blocks, blocks, left),
        check_vma=False,
    )
```
